32 devices in a mesh: group: 2 (over y), expert: 4 (over z), tensor: 4 (over x, core).
Axes of the slice: x: 2, y: 2, z: 4, core: 2. Of those that a mesh axis runs over, the one named last changes fastest.
Arguments:
- residual: float32 [256, 3584], P(('group', 'expert')), parts along dimension 0, may hold values from -30 to 30
- attention_part: bfloat16 [4, 256, 3584], P('tensor', ('group', 'expert')), parts along dimension 1, may hold values from -2.5 to 2.5
- norm_gain: float32 [3584], replicated, may hold values from 0.25 to 1.75
- expert_ids: int32 [256, 2], P(('group', 'expert')), parts along dimension 0, may hold values from 0 to 3, all different within a row; in each aligned block of 32 rows (0 to 31, 32 to 63, ...) at most 17 rows name the same one
- gate_weights: float32 [256, 2], P(('group', 'expert')), parts along dimension 0, may hold values from 0.1 to 0.9
- w_gate: bfloat16 [4, 3584, 1024], P('expert', None, 'tensor'), may hold values from -0.09375 to 0.09375
- w_up: bfloat16 [4, 3584, 1024], P('expert', None, 'tensor'), may hold values from -0.09375 to 0.09375
- w_down: bfloat16 [4, 1024, 3584], P('expert', 'tensor'), may hold values from -0.1875 to 0.1875
Outputs:
- layer_out: float32 [256, 3584], P(('group', 'expert'), 'tensor'), parts along dimension 0
The draws below stay inside these ranges and needn't reach their ends.
There are 2 independent parts, one for each index of `group`. The reference program is written for one: setup_inputs(seed, part) draws one part's arguments, and reference() takes and returns one part's arrays. A program takes and returns all parts, laid end to end along the dimension named above; an argument that names none is the same for every part. Nothing has to cross between parts.
Inputs may be any that keep to these rules, and one draw needn't show every extreme that they name: `expert_ids`: each row names 2 different experts; within the rows of one index of the expert axis (aligned blocks of 32 rows) no expert is named by more than 17 rows, a bound that some block reaches.
All inputs are finite; a program needn't handle non-finite values.
Results may differ from the reference program's by a relative error of at most 0.0055.
Values may be sent and summed in bfloat16 or wider, within the bound.
No kernel may reach another device: no remote copies, remote signals or barrier semaphores. Data moves between devices by JAX's collectives and lax.ppermute only.
A program may use at most 64 MiB of HBM per device.

```python
import math
import jax
import jax.numpy as jnp
import numpy as np
from jax import lax

D = 3584
FFE = 1024
R_DEV = 32
CAP = 17
EXPERTS = 4
TOP = 2
ROWS = 128
N_EXPERT = 4
N_TENSOR = 4


def draw_residual(key, part):
    key = jax.random.fold_in(key, 7)
    key_base, key_rows, key_cols = jax.random.split(key, 3)
    values = jnp.clip(jax.random.normal(key_base, (ROWS, D), jnp.float32), -4.0, 4.0)
    spread = 2.0
    row_scale = jnp.exp(jax.random.uniform(key_rows, (ROWS, 1), jnp.float32, -1.0, 1.0) * math.log(spread))
    col_scale = jnp.exp(jax.random.uniform(key_cols, (1, D), jnp.float32, -1.0, 1.0) * math.log(spread))
    column_ramp = 0.6 + 1.2 * jnp.arange(D, dtype=jnp.float32)[None, :] / D
    return jnp.clip(values * row_scale * col_scale * column_ramp, -30.0, 30.0)


def levels(stream_key, shape, cuts, least, top_value):
    gain, own = 1.0, jax.random.fold_in(stream_key, 6)
    for axis_at, blocks in cuts:
        steps = jnp.exp(jax.random.uniform(jax.random.fold_in(own, axis_at), (blocks,), jnp.float32, least / len(cuts), top_value / len(cuts)))
        gain = gain * jnp.repeat(steps, shape[axis_at] // blocks).reshape([-1 if axis == axis_at else 1 for axis in range(len(shape))])
    return gain


def routed_block(own_key, own, number, rows, amount, top, limit, lean):
    ranking = jax.random.permutation(own_key, amount)
    packed, ordinary = load_shares(amount, rows * top, limit, lean, True), load_shares(amount, rows * top, limit, lean, False)
    places = jnp.arange(amount)

    def named(tallies, offset_by):
        used = int((tallies > 0).sum())
        fixed = max(1, used // 4)
        shifted = fixed + (places - fixed + offset_by * (used - fixed)) % max(1, amount - fixed)
        return jnp.zeros((amount,), jnp.int32).at[ranking[jnp.where(places < fixed, places, shifted)]].set(jnp.asarray(tallies, jnp.int32))

    tallies = jnp.where(number % 4 == 0, named(packed, number // 4), named(ordinary, number - number // 4 - 1))
    mixed = jax.random.permutation(jax.random.fold_in(own, 3), amount)
    donor, taker = mixed[0:amount // 2 * 2:2], mixed[1:amount // 2 * 2:2]
    room = jnp.minimum(tallies[donor] - 1, limit - tallies[taker]) // 2
    room = jnp.where((donor == ranking[0]) | (taker == ranking[0]) | (tallies[taker] == 0), 0, jnp.maximum(room, 0))
    shifted = jax.random.randint(jax.random.fold_in(own, 4), (amount // 2,), 0, 1 << 20) % (room + 1)
    tallies = tallies.at[donor].add(-shifted).at[taker].add(shifted)
    items = jnp.searchsorted(jnp.cumsum(tallies), jnp.arange(rows * top), side="right").astype(jnp.int32)
    listing = items.reshape(top, rows).T
    listing = listing[jax.random.permutation(jax.random.fold_in(own, 1), rows)]
    offset_by = jax.random.randint(jax.random.fold_in(own, 2), (rows, 1), 0, top)
    return jnp.take_along_axis(listing, (jnp.arange(top)[None, :] + offset_by) % top, axis=1)


def load_shares(count, total, most, lean, full):
    loads = [(1 << 20) // math.isqrt(standing ** lean) + 1 for standing in range(1, count + 1)]
    largest = most if full else min(most, max(-(-total // count), total * loads[0] // sum(loads)))
    least = 1 if total - largest >= count - 1 else 0
    counts, surplus = [largest] + [least] * (count - 1), total - largest - least * (count - 1)
    while surplus > 0:
        candidates = [i for i in range(1, count) if counts[i] < largest] or [i for i in range(1, count) if counts[i] < most]
        pool, remaining = sum([loads[i] for i in candidates]), surplus
        for i in candidates:
            addition = min(most - counts[i], max(1, remaining * loads[i] // pool), surplus)
            counts[i] = counts[i] + addition
            surplus = surplus - addition
    return np.array(counts)


def normal_values(rng, dims, deviation, reach, cuts=(), kind=jnp.bfloat16):
    result = jax.random.normal(rng, dims, jnp.float32) * deviation
    if len(cuts) > 0:
        result = levels(rng, dims, cuts, -0.22, 0.18) * result
    return jnp.clip(result, min=-reach, max=reach).astype(kind)


def setup_inputs(seed: int = 0, part: int = 0) -> dict:
    streams_of = jax.random.split(jax.random.key(seed), 9)
    part_keys = jax.random.split(jax.random.fold_in(streams_of[8], part), 9)
    residual = draw_residual(jax.random.fold_in(jax.random.fold_in(streams_of[8], part), 71), part)
    attention_part = normal_values(part_keys[1], (N_TENSOR, ROWS, D), 0.4, 2.5, ((0, 4), (1, 4)))
    norm_gain = jnp.clip(1.0 + 0.15 * jax.random.normal(streams_of[2], (D,), jnp.float32), 0.25, 1.75)
    expert_ids_keys = jax.random.split(jax.random.fold_in(part_keys[3], 1), ROWS // R_DEV)
    expert_ids_turns = jax.random.permutation(jax.random.fold_in(part_keys[3], 3), ROWS // R_DEV)
    expert_ids = jax.vmap(lambda own, number: routed_block(jax.random.fold_in(part_keys[3], 2), own, number, R_DEV, EXPERTS, TOP, CAP, 2))(expert_ids_keys, expert_ids_turns).reshape((ROWS, TOP))
    gate_weights = jnp.clip(0.1 + 0.79999997 * jax.random.uniform(part_keys[4], (ROWS, TOP), jnp.float32) ** levels(part_keys[4], (ROWS, TOP), ((0, 4),), -0.2, 0.2), 0.1, 0.9)
    w_gate = normal_values(streams_of[5], (EXPERTS, D, FFE), D ** -0.5, 0.09375, ((0, 4), (2, 4)))
    w_up = normal_values(streams_of[6], (EXPERTS, D, FFE), D ** -0.5, 0.09375, ((0, 4), (2, 4)))
    w_down = normal_values(streams_of[7], (EXPERTS, FFE, D), FFE ** -0.5, 0.1875, ((0, 4), (1, 4)))
    return dict(residual=residual, attention_part=attention_part, norm_gain=norm_gain, expert_ids=expert_ids, gate_weights=gate_weights, w_gate=w_gate, w_up=w_up, w_down=w_down)


EPSILON = 1e-06

def one_expert(operands):
    inputs, gate_weight, up_weight, down_weight = operands
    gated = jnp.dot(inputs, gate_weight, preferred_element_type=jnp.float32)
    upward = jnp.dot(inputs, up_weight, preferred_element_type=jnp.float32)
    active = (jax.nn.silu(gated) * upward).astype(jnp.bfloat16)
    blocked = active.reshape(active.shape[0], N_TENSOR, FFE // N_TENSOR).astype(jnp.float32)
    down_blocks = down_weight.reshape(N_TENSOR, FFE // N_TENSOR, D).astype(jnp.float32)
    partial_value = jnp.einsum('sbf,bfd->bsd', blocked, down_blocks, precision=lax.Precision.HIGHEST)
    rounded = lax.optimization_barrier(partial_value.astype(jnp.bfloat16))
    return lax.optimization_barrier(jnp.sum(rounded.astype(jnp.float32), axis=0))

def reference(residual, attention_part, norm_gain, expert_ids, gate_weights, w_gate, w_up, w_down):
    attention = lax.optimization_barrier(jnp.sum(attention_part.astype(jnp.float32), axis=0))
    hidden = residual + attention
    inverse = lax.rsqrt(lax.optimization_barrier(jnp.mean(hidden * hidden, axis=1, keepdims=True)) + EPSILON)
    normed = (hidden * inverse * norm_gain).astype(jnp.bfloat16)
    grouped = expert_ids.reshape(N_EXPERT, R_DEV * TOP)
    onehot = (grouped[:, :, None] == jnp.arange(EXPERTS, dtype=jnp.int32)[None, None, :]).astype(jnp.int32)
    before = jnp.cumsum(onehot, axis=1) - onehot
    position = lax.optimization_barrier(jnp.sum(before * onehot, axis=2)).astype(jnp.int32)
    sender = jnp.arange(N_EXPERT, dtype=jnp.int32)[:, None]
    slot_index = (grouped * (N_EXPERT * CAP) + sender * CAP + position).reshape(-1).astype(jnp.int32)
    slot_total = EXPERTS * N_EXPERT * CAP
    row_owner = jnp.arange(ROWS * TOP, dtype=jnp.int32) // TOP
    slot_rows = jnp.full((slot_total,), ROWS, jnp.int32).at[slot_index].set(row_owner)
    padded = jnp.concatenate([normed, jnp.zeros((1, D), jnp.bfloat16)], axis=0)
    buffers = padded[slot_rows].reshape(EXPERTS, N_EXPERT * CAP, D)
    results = lax.map(one_expert, (buffers, w_gate, w_up, w_down))
    picked = results.reshape(slot_total, D)[slot_index].reshape(ROWS, TOP, D)
    return hidden + lax.optimization_barrier(jnp.sum(gate_weights[:, :, None] * picked, axis=1))
```

```python
import jax
import jax.numpy as jnp
from jax import lax
from jax.sharding import PartitionSpec as P

CAP = 17
EPSILON = 1e-06


def xor_permute(value, axis, step):
    count = lax.axis_size(axis)
    return lax.ppermute(value, axis, [(i, i ^ step) for i in range(count)])


def split_pair(value):
    high = value.astype(jnp.bfloat16)
    return high, (value - high.astype(jnp.float32)).astype(jnp.bfloat16)


def local(residual, attention_part, norm_gain, expert_ids, gate_weights, w_gate, w_up, w_down):
    rows, features = residual.shape
    tensor_count = lax.axis_size("tensor")
    expert_count = lax.axis_size("expert")
    tensor = lax.axis_index("tensor")
    expert = lax.axis_index("expert")
    quarter = features // tensor_count
    outer = tensor_count // 2
    side = tensor % 2

    def strips(value):
        shaped = value.reshape(value.shape[0], outer, 2, quarter)
        return lax.dynamic_index_in_dim(shaped, side, 2, keepdims=False)

    part = attention_part[0]
    near = xor_permute(part, "tensor", 1)
    chip = strips(part.astype(jnp.float32) + near.astype(jnp.float32))
    chip_sent = chip.astype(jnp.bfloat16)
    far = [xor_permute(chip_sent, "tensor", 2 * step) for step in range(1, outer)]

    relative = expert_ids ^ expert
    blocks = jnp.arange(expert_count, dtype=jnp.int32)
    chosen = relative[:, :, None] == blocks[None, None, :]
    named = jnp.any(chosen, axis=1)
    gates = jnp.sum(jnp.where(chosen, gate_weights[:, :, None], 0.0), axis=1)
    below = jnp.arange(rows)[:, None] > jnp.arange(rows)[None, :]
    position = jnp.dot(below.astype(jnp.bfloat16), named.astype(jnp.bfloat16), preferred_element_type=jnp.float32)
    slots = jnp.arange(CAP, dtype=jnp.float32)
    table = (position.T[:, None, :] == slots[None, :, None]) & named.T[:, None, :]
    mixing = jnp.where(table, gates.T[:, None, :], 0.0).reshape(expert_count * CAP, rows)
    table = table.astype(jnp.bfloat16)

    hidden = strips(residual) + chip
    for value in far:
        hidden = hidden + value.astype(jnp.float32)
    squares = jnp.sum(hidden * hidden, axis=(1, 2))
    high, low = split_pair(squares)
    extra = jnp.zeros((rows, 128), jnp.bfloat16).at[:, 0].set(high).at[:, 1].set(low)
    gained = (hidden * strips(norm_gain[None])).astype(jnp.bfloat16).reshape(rows, outer * quarter)
    sent = jnp.concatenate([gained, extra], axis=1)
    arrived = []
    for step in range(expert_count):
        block = jnp.dot(table[step], sent, preferred_element_type=jnp.float32).astype(jnp.bfloat16)
        arrived.append(xor_permute(block, "expert", step) if step else block)
    other = [xor_permute(block, "tensor", 1) for block in arrived]
    arrived, other = jnp.concatenate(arrived, axis=0), jnp.concatenate(other, axis=0)

    def columns(value):
        return value[:, : outer * quarter].reshape(-1, outer, quarter)

    first = jnp.where(side == 0, arrived, other)
    second = jnp.where(side == 0, other, arrived)
    inputs = jnp.stack([columns(first), columns(second)], axis=2).reshape(-1, features)
    tails = (arrived[:, outer * quarter :].astype(jnp.float32), other[:, outer * quarter :].astype(jnp.float32))
    total = tails[0][:, 0] + tails[0][:, 1] + tails[1][:, 0] + tails[1][:, 1]
    inverse = lax.rsqrt(total / features + EPSILON)[:, None]
    gated = jnp.dot(inputs, w_gate[0], preferred_element_type=jnp.float32) * inverse
    upward = jnp.dot(inputs, w_up[0], preferred_element_type=jnp.float32) * inverse
    active = (jax.nn.silu(gated) * upward).astype(jnp.bfloat16)
    produced = jnp.dot(active, w_down[0], preferred_element_type=jnp.float32)

    def own_columns(index):
        return lax.dynamic_slice_in_dim(produced, index * quarter, quarter, 1)

    reduced = own_columns(tensor)
    for step in range(1, tensor_count):
        piece = own_columns(tensor ^ step).astype(jnp.bfloat16)
        reduced = reduced + xor_permute(piece, "tensor", step).astype(jnp.float32)
    reduced = reduced.astype(jnp.bfloat16).reshape(expert_count, CAP, quarter)
    returned = [xor_permute(reduced[k], "expert", k) if k else reduced[k] for k in range(expert_count)]
    returned = jnp.concatenate(returned, axis=0)
    high, low = split_pair(mixing)
    dims = (((0,), (0,)), ((), ()))
    combined = lax.dot_general(high, returned, dims, preferred_element_type=jnp.float32)
    combined = combined + lax.dot_general(low, returned, dims, preferred_element_type=jnp.float32)
    return lax.dynamic_index_in_dim(hidden, tensor // 2, 1, keepdims=False) + combined


def solution(mesh):
    in_specs = (
        P(("group", "expert"), None),
        P("tensor", ("group", "expert"), None),
        P(),
        P(("group", "expert"), None),
        P(("group", "expert"), None),
        P("expert", None, "tensor"),
        P("expert", None, "tensor"),
        P("expert", "tensor", None),
    )
    out_specs = P(("group", "expert"), "tensor")
    return jax.shard_map(local, mesh=mesh, in_specs=in_specs, out_specs=out_specs, check_vma=False)
```

```python
import functools

import jax
import jax.numpy as jnp
from jax import lax
from jax.experimental import pallas as pl
from jax.experimental.pallas import tpu as pltpu
from jax.sharding import PartitionSpec as P

CAP = 17
EPSILON = 1e-06
LANES = 128
MAIN = 16
FLOPS = 4 << 30
BF16, F32 = jnp.bfloat16, jnp.float32


def xor_permute(value, axis, step):
    count = lax.axis_size(axis)
    return lax.ppermute(value, axis, [(i, i ^ step) for i in range(count)])


def split_pair(value):
    high = value.astype(jnp.bfloat16)
    return high, (value - high.astype(jnp.float32)).astype(jnp.bfloat16)


def call(kernel, outs, *args, scratch=(), vmem=8 << 20, flops=FLOPS, name=None):
    vmem_spec = pl.BlockSpec(memory_space=pltpu.VMEM)
    moved = sum(a.size * a.dtype.itemsize for a in (*args, *outs))
    return pl.pallas_call(
        kernel,
        out_shape=tuple(outs),
        in_specs=[vmem_spec] * len(args),
        out_specs=(vmem_spec,) * len(outs),
        scratch_shapes=list(scratch),
        compiler_params=pltpu.CompilerParams(vmem_limit_bytes=vmem),
        cost_estimate=pl.CostEstimate(flops=flops, bytes_accessed=moved, transcendentals=0),
        name=name,
    )(*args)


def out(shape, dtype):
    return jax.ShapeDtypeStruct(shape, dtype)


def iota(shape, dim):
    return lax.broadcasted_iota(jnp.int32, shape, dim)


def onehot(mask):
    return jnp.where(mask, 1.0, 0.0)


def dot(left, right, contract=((1,), (0,))):
    return lax.dot_general(left, right, (contract, ((), ())), preferred_element_type=F32)


def strip(index, quarter):
    return pl.ds(pl.multiple_of(index * quarter, LANES), quarter)


def constant_kernel(rows, before_ref, spread_ref):
    before_ref[...] = onehot(iota((rows, rows), 0) < iota((rows, rows), 1)).astype(BF16)
    shape = spread_ref.shape
    spread_ref[...] = onehot(iota(shape, 0) == iota(shape, 1) % rows).astype(BF16)


def table_kernel(experts, rows, chunks, before_ref, spread_ref, ids_ref, gates_ref, table_ref, tails_ref, high_ref, low_ref):
    expert = lax.axis_index("expert")
    relative = ids_ref[...] ^ expert
    gates = gates_ref[...]
    kinds = iota((8, rows), 0)
    named, gate = jnp.zeros((8, rows), jnp.bool_), jnp.zeros((8, rows), F32)
    for choice in range(relative.shape[0]):
        hit = relative[choice : choice + 1] == kinds
        named = named | hit
        gate = gate + jnp.where(hit, gates[choice : choice + 1], 0.0)
    position = dot(onehot(named).astype(BF16), before_ref[...])
    position = jnp.where(named, position, -1.0)
    slot = iota((MAIN, rows), 0).astype(F32)
    pieces = [onehot(position[k : k + 1] == slot) for k in range(experts)]
    tail = onehot(position == float(MAIN))
    rest = table_ref.shape[0] - experts * MAIN - 8
    table = jnp.concatenate([*pieces, tail, jnp.zeros((rest, rows), F32)], axis=0)
    table_ref[...] = table.astype(BF16)
    wide = jnp.concatenate([jnp.broadcast_to(tail[k : k + 1], (MAIN, rows)) for k in range(experts)], axis=0)
    spread = dot(wide.astype(BF16), spread_ref[...])
    shape = (experts * MAIN, rows * chunks)
    tails_ref[...] = jnp.where(iota(shape, 0) % MAIN == iota(shape, 1) // rows, spread, 0.0).astype(BF16)
    for k in range(experts):
        last = jnp.where(iota((8, rows), 0) == k, tail, 0.0)
        mixing = jnp.concatenate([pieces[k], last], axis=0) * gate[k : k + 1]
        high, low = split_pair(mixing)
        high_ref[k], low_ref[k] = high, low


def chip_kernel(quarter, part_ref, near_ref, after_ref, chip_ref, sent_ref):
    del after_ref
    side = lax.axis_index("tensor") % 2
    for o in range(2):
        columns = strip(2 * o + side, quarter)
        total = part_ref[:, columns].astype(F32) + near_ref[:, columns].astype(F32)
        chip_ref[:, o * quarter : (o + 1) * quarter] = total
        sent_ref[:, o * quarter : (o + 1) * quarter] = total.astype(BF16)


def dispatch_kernel(quarter, experts, residual_ref, chip_ref, far_ref, gain_ref, table_ref, tails_ref, hidden_ref, *block_refs):
    tensor = lax.axis_index("tensor")
    side = tensor % 2
    rows = chip_ref.shape[0]
    squares = jnp.zeros((rows, 1), F32)
    gained = []
    for o in range(2):
        here = slice(o * quarter, (o + 1) * quarter)
        columns = strip(2 * o + side, quarter)
        hidden = residual_ref[:, columns] + chip_ref[:, here] + far_ref[:, here].astype(F32)
        squares = squares + jnp.sum(hidden * hidden, axis=1, keepdims=True)
        gained.append((hidden * gain_ref[:, columns]).astype(BF16))

        @pl.when(o == tensor // 2)
        def _():
            hidden_ref[...] = hidden

    table = table_ref[...]
    main = table[: experts * MAIN]
    lanes = jnp.sum(jnp.where(iota((rows, rows), 0) == iota((rows, rows), 1), squares, 0.0), axis=0, keepdims=True)
    high = lanes.astype(BF16).astype(F32)
    pick = iota((MAIN, rows), 0)
    pair = jnp.where(pick == 0, high, jnp.where(pick == 1, lanes - high, 0.0)).astype(BF16)
    slots = dot(pair, table, ((1,), (1,)))
    for o in range(2):
        picked = dot(main, gained[o]).astype(BF16)
        for k in range(experts):
            block_refs[k][:, o * quarter : (o + 1) * quarter] = picked[k * MAIN : (k + 1) * MAIN]
    parts = [g[:, i * LANES : (i + 1) * LANES] for g in gained for i in range(quarter // LANES)]
    tile = dot(tails_ref[...], jnp.concatenate(parts, axis=0))
    row = iota(tile.shape, 0) % MAIN
    tile = jnp.where(row == MAIN - 2, slots[0:1], jnp.where(row == MAIN - 1, slots[1:2], tile)).astype(BF16)
    for k in range(experts):
        block_refs[k][:, 2 * quarter :] = tile[k * MAIN : (k + 1) * MAIN]


def pack_kernel(experts, *refs):
    for ref, k in zip(refs, reversed(range(experts))):
        refs[-1][k * MAIN : (k + 1) * MAIN] = ref[...]


def project(quarter, experts, ref, which, gate_ref, up_ref):
    chunks = 2 * quarter // LANES
    shape = (chunks * MAIN, experts * MAIN)
    block = iota(shape, 0) % MAIN
    spread = onehot((iota(shape, 1) == block * MAIN + iota(shape, 0) // MAIN) & (block < experts)).astype(BF16)
    last = dot(spread, ref[:, 2 * quarter :]).astype(BF16)
    gated = upward = 0.0
    per = quarter // LANES
    for o in range(2):
        tails = jnp.concatenate([last[j * MAIN : (j + 1) * MAIN] for j in range(o * per, (o + 1) * per)], axis=1)
        inputs = jnp.concatenate([ref[:, o * quarter : (o + 1) * quarter], tails], axis=0)
        here = strip(2 * o + which, quarter)
        gated = gated + dot(inputs, gate_ref[0, here, :])
        upward = upward + dot(inputs, up_ref[0, here, :])
    return gated, upward


def own_kernel(quarter, experts, own_ref, gate_ref, up_ref, gated_ref, upward_ref):
    side = lax.axis_index("tensor") % 2
    gated_ref[...], upward_ref[...] = project(quarter, experts, own_ref, side, gate_ref, up_ref)


def other_kernel(
    quarter, experts, own_ref, other_ref, gated_ref, upward_ref, gate_ref, up_ref, down_ref, active_ref, sent_ref
):
    side = lax.axis_index("tensor") % 2
    main, features = experts * MAIN, 4 * quarter
    lane = iota((1, LANES), 1)
    total = jnp.zeros((1, LANES), F32)
    for ref in (own_ref, other_ref):
        for k in range(experts):
            pair = ref[k * MAIN : (k + 1) * MAIN, 2 * quarter :].astype(F32)
            value = pair[MAIN - 2 : MAIN - 1] + pair[MAIN - 1 : MAIN]
            total = total + jnp.where((lane // MAIN == k) | (lane == main + k), value, 0.0)
    gated, upward = project(quarter, experts, other_ref, 1 - side, gate_ref, up_ref)
    gated, upward = gated + gated_ref[...], upward + upward_ref[...]
    shape = (gated.shape[0], LANES)
    column = jnp.sum(jnp.where(iota(shape, 0) == iota(shape, 1), total, 0.0), axis=1, keepdims=True)
    inverse = lax.rsqrt(column / features + EPSILON)
    gated, upward = gated * inverse, upward * inverse
    active = (gated / (1.0 + jnp.exp(-gated)) * upward).astype(BF16)
    active_ref[...] = active
    for o in range(2):
        value = dot(active, down_ref[0, :, strip(2 * o + 1 - side, quarter)]).astype(BF16)
        sent_ref[:, o * quarter : (o + 1) * quarter] = value[: sent_ref.shape[0]]


def kept_kernel(quarter, active_ref, down_ref, kept_ref):
    side = lax.axis_index("tensor") % 2
    for o in range(2):
        value = dot(active_ref[...], down_ref[0, :, strip(2 * o + side, quarter)]).astype(BF16)
        kept_ref[:, o * quarter : (o + 1) * quarter] = value[: kept_ref.shape[0]]


def near_kernel(quarter, kept_ref, near_ref, own_ref, sent_ref):
    o = lax.axis_index("tensor") // 2
    for ref, index in ((own_ref, o), (sent_ref, 1 - o)):
        columns = strip(index, quarter)
        ref[...] = (kept_ref[:, columns].astype(F32) + near_ref[:, columns].astype(F32)).astype(ref.dtype)


def far_kernel(experts, own_ref, far_ref, *block_refs):
    total = own_ref[...] + far_ref[...].astype(F32)
    main = experts * MAIN
    for k in range(experts):
        block = jnp.concatenate([total[k * MAIN : (k + 1) * MAIN], total[main : main + 8]], axis=0)
        block_refs[k][...] = block.astype(BF16)


def combine_kernel(experts, hidden_ref, high_ref, low_ref, *refs):
    total = hidden_ref[...]
    for ref, k in zip(refs, reversed(range(experts))):
        value = ref[...]
        total = total + dot(high_ref[k], value, ((0,), (0,))) + dot(low_ref[k], value, ((0,), (0,)))
    refs[-1][...] = total


def local_kernels(residual, attention_part, norm_gain, expert_ids, gate_weights, w_gate, w_up, w_down):
    rows, features = residual.shape
    experts = lax.axis_size("expert")
    quarter = features // 4
    width = 2 * quarter
    chunks = width // LANES
    steps = range(1, experts)
    part = attention_part[0]
    near = xor_permute(part, "tensor", 1)
    before, spread = call(
        functools.partial(constant_kernel, rows), (out((rows, rows), BF16), out((rows, rows * chunks), BF16))
    )
    mix = out((experts, MAIN + 8, rows), BF16)
    table, tails, high, low = call(
        functools.partial(table_kernel, experts, rows, chunks),
        (out((LANES, rows), BF16), out((experts * MAIN, rows * chunks), BF16), mix, mix),
        before,
        spread,
        expert_ids.T,
        gate_weights.T,
    )
    chip, chip_sent = call(
        functools.partial(chip_kernel, quarter), (out((rows, width), F32), out((rows, width), BF16)), part, near, high
    )
    far = xor_permute(chip_sent, "tensor", 2)
    block = out((MAIN, width + LANES), BF16)
    hidden, *blocks = call(
        functools.partial(dispatch_kernel, quarter, experts),
        (out((rows, quarter), F32), *[block] * experts),
        residual,
        chip,
        far,
        norm_gain[None],
        table,
        tails,
    )
    arrived = [*[xor_permute(blocks[k], "expert", k) for k in reversed(steps)], blocks[0]]
    packed = out((experts * MAIN, width + LANES), BF16)
    (arrived,) = call(functools.partial(pack_kernel, experts), (packed,), *arrived, flops=0)
    other = xor_permute(arrived, "tensor", 1)
    used, slots = experts * MAIN + 8, (experts + 1) * MAIN
    hidden_count = w_gate.shape[2]
    sums = out((slots, hidden_count), F32)
    gated, upward = call(functools.partial(own_kernel, quarter, experts), (sums, sums), arrived, w_gate, w_up)
    active, sent = call(
        functools.partial(other_kernel, quarter, experts),
        (out((slots, hidden_count), BF16), out((used, width), BF16)),
        arrived,
        other,
        gated,
        upward,
        w_gate,
        w_up,
        w_down,
    )
    (kept,) = call(functools.partial(kept_kernel, quarter), (out((used, width), BF16),), active, w_down)
    near = xor_permute(sent, "tensor", 1)
    own, sent = call(
        functools.partial(near_kernel, quarter), (out((used, quarter), F32), out((used, quarter), BF16)), kept, near
    )
    far = xor_permute(sent, "tensor", 2)
    blocks = call(functools.partial(far_kernel, experts), [out((MAIN + 8, quarter), BF16)] * experts, own, far)
    blocks = [*[xor_permute(blocks[k], "expert", k) for k in reversed(steps)], blocks[0]]
    (result,) = call(functools.partial(combine_kernel, experts), (out((rows, quarter), F32),), hidden, high, low, *blocks)
    return result


def local(residual, *others):
    rows, features = residual.shape
    fits = lax.axis_size("tensor") == 4 and lax.axis_size("expert") == 4 and rows % 16 == 0 and rows <= LANES
    quarter = features // 4
    if fits and quarter % LANES == 0 and 2 * quarter // LANES <= MAIN - 2:
        return local_kernels(residual, *others)
    return local_general(residual, *others)


def local_general(residual, attention_part, norm_gain, expert_ids, gate_weights, w_gate, w_up, w_down):
    rows, features = residual.shape
    tensor_count = lax.axis_size("tensor")
    expert_count = lax.axis_size("expert")
    tensor = lax.axis_index("tensor")
    expert = lax.axis_index("expert")
    quarter = features // tensor_count
    outer = tensor_count // 2
    side = tensor % 2

    def strips(value):
        shaped = value.reshape(value.shape[0], outer, 2, quarter)
        return lax.dynamic_index_in_dim(shaped, side, 2, keepdims=False)

    part = attention_part[0]
    near = xor_permute(part, "tensor", 1)
    chip = strips(part.astype(jnp.float32) + near.astype(jnp.float32))
    chip_sent = chip.astype(jnp.bfloat16)
    far = [xor_permute(chip_sent, "tensor", 2 * step) for step in range(1, outer)]

    relative = expert_ids ^ expert
    blocks = jnp.arange(expert_count, dtype=jnp.int32)
    chosen = relative[:, :, None] == blocks[None, None, :]
    named = jnp.any(chosen, axis=1)
    gates = jnp.sum(jnp.where(chosen, gate_weights[:, :, None], 0.0), axis=1)
    below = jnp.arange(rows)[:, None] > jnp.arange(rows)[None, :]
    position = jnp.dot(below.astype(jnp.bfloat16), named.astype(jnp.bfloat16), preferred_element_type=jnp.float32)
    slots = jnp.arange(CAP, dtype=jnp.float32)
    table = (position.T[:, None, :] == slots[None, :, None]) & named.T[:, None, :]
    mixing = jnp.where(table, gates.T[:, None, :], 0.0).reshape(expert_count * CAP, rows)
    table = table.astype(jnp.bfloat16)

    hidden = strips(residual) + chip
    for value in far:
        hidden = hidden + value.astype(jnp.float32)
    squares = jnp.sum(hidden * hidden, axis=(1, 2))
    high, low = split_pair(squares)
    extra = jnp.zeros((rows, 128), jnp.bfloat16).at[:, 0].set(high).at[:, 1].set(low)
    gained = (hidden * strips(norm_gain[None])).astype(jnp.bfloat16).reshape(rows, outer * quarter)
    sent = jnp.concatenate([gained, extra], axis=1)
    arrived = []
    for step in range(expert_count):
        block = jnp.dot(table[step], sent, preferred_element_type=jnp.float32).astype(jnp.bfloat16)
        arrived.append(xor_permute(block, "expert", step) if step else block)
    other = [xor_permute(block, "tensor", 1) for block in arrived]
    arrived, other = jnp.concatenate(arrived, axis=0), jnp.concatenate(other, axis=0)

    def columns(value):
        return value[:, : outer * quarter].reshape(-1, outer, quarter)

    first = jnp.where(side == 0, arrived, other)
    second = jnp.where(side == 0, other, arrived)
    inputs = jnp.stack([columns(first), columns(second)], axis=2).reshape(-1, features)
    tails = (arrived[:, outer * quarter :].astype(jnp.float32), other[:, outer * quarter :].astype(jnp.float32))
    total = tails[0][:, 0] + tails[0][:, 1] + tails[1][:, 0] + tails[1][:, 1]
    inverse = lax.rsqrt(total / features + EPSILON)[:, None]
    gated = jnp.dot(inputs, w_gate[0], preferred_element_type=jnp.float32) * inverse
    upward = jnp.dot(inputs, w_up[0], preferred_element_type=jnp.float32) * inverse
    active = (jax.nn.silu(gated) * upward).astype(jnp.bfloat16)
    produced = jnp.dot(active, w_down[0], preferred_element_type=jnp.float32)

    def own_columns(index):
        return lax.dynamic_slice_in_dim(produced, index * quarter, quarter, 1)

    reduced = own_columns(tensor)
    for step in range(1, tensor_count):
        piece = own_columns(tensor ^ step).astype(jnp.bfloat16)
        reduced = reduced + xor_permute(piece, "tensor", step).astype(jnp.float32)
    reduced = reduced.astype(jnp.bfloat16).reshape(expert_count, CAP, quarter)
    returned = [xor_permute(reduced[k], "expert", k) if k else reduced[k] for k in range(expert_count)]
    returned = jnp.concatenate(returned, axis=0)
    high, low = split_pair(mixing)
    dims = (((0,), (0,)), ((), ()))
    combined = lax.dot_general(high, returned, dims, preferred_element_type=jnp.float32)
    combined = combined + lax.dot_general(low, returned, dims, preferred_element_type=jnp.float32)
    return lax.dynamic_index_in_dim(hidden, tensor // 2, 1, keepdims=False) + combined


def solution(mesh):
    in_specs = (
        P(("group", "expert"), None),
        P("tensor", ("group", "expert"), None),
        P(),
        P(("group", "expert"), None),
        P(("group", "expert"), None),
        P("expert", None, "tensor"),
        P("expert", None, "tensor"),
        P("expert", "tensor", None),
    )
    out_specs = P(("group", "expert"), "tensor")
    return jax.shard_map(local, mesh=mesh, in_specs=in_specs, out_specs=out_specs, check_vma=False)
```

```python
import functools

import jax
import jax.numpy as jnp
from jax import lax
from jax.experimental import pallas as pl
from jax.experimental.pallas import tpu as pltpu
from jax.sharding import PartitionSpec as P

CAP = 17
EPSILON = 1e-06
LANES = 128
MAIN = 16
FLOPS = 4 << 30
BF16, F32 = jnp.bfloat16, jnp.float32


def xor_permute(value, axis, step):
    count = lax.axis_size(axis)
    return lax.ppermute(value, axis, [(i, i ^ step) for i in range(count)])


def split_pair(value):
    high = value.astype(jnp.bfloat16)
    return high, (value - high.astype(jnp.float32)).astype(jnp.bfloat16)


def call(kernel, outs, *args, scratch=(), vmem=8 << 20, flops=FLOPS, name=None):
    vmem_spec = pl.BlockSpec(memory_space=pltpu.VMEM)
    moved = sum(a.size * a.dtype.itemsize for a in (*args, *outs))
    return pl.pallas_call(
        kernel,
        out_shape=tuple(outs),
        in_specs=[vmem_spec] * len(args),
        out_specs=(vmem_spec,) * len(outs),
        scratch_shapes=list(scratch),
        compiler_params=pltpu.CompilerParams(vmem_limit_bytes=vmem),
        cost_estimate=pl.CostEstimate(flops=flops, bytes_accessed=moved, transcendentals=0),
        name=name,
    )(*args)


def out(shape, dtype):
    return jax.ShapeDtypeStruct(shape, dtype)


def iota(shape, dim):
    return lax.broadcasted_iota(jnp.int32, shape, dim)


def onehot(mask):
    return jnp.where(mask, 1.0, 0.0)


def dot(left, right, contract=((1,), (0,))):
    return lax.dot_general(left, right, (contract, ((), ())), preferred_element_type=F32)


def strip(index, quarter):
    return pl.ds(pl.multiple_of(index * quarter, LANES), quarter)


def constant_kernel(rows, before_ref, spread_ref):
    before_ref[...] = onehot(iota((rows, rows), 0) < iota((rows, rows), 1)).astype(BF16)
    shape = spread_ref.shape
    spread_ref[...] = onehot(iota(shape, 0) == iota(shape, 1) % rows).astype(BF16)


def table_kernel(experts, rows, chunks, before_ref, spread_ref, ids_ref, gates_ref, table_ref, tails_ref, mixing_ref):
    expert = lax.axis_index("expert")
    relative = ids_ref[...] ^ expert
    gates = gates_ref[...]
    kinds = iota((8, rows), 0)
    named, gate = jnp.zeros((8, rows), jnp.bool_), jnp.zeros((8, rows), F32)
    for choice in range(relative.shape[0]):
        hit = relative[choice : choice + 1] == kinds
        named = named | hit
        gate = gate + jnp.where(hit, gates[choice : choice + 1], 0.0)
    position = dot(onehot(named).astype(BF16), before_ref[...])
    position = jnp.where(named, position, -1.0)
    slot = iota((MAIN, rows), 0).astype(F32)
    pieces = [onehot(position[k : k + 1] == slot) for k in range(experts)]
    tail = onehot(position == float(MAIN))
    rest = table_ref.shape[0] - experts * MAIN - 8
    table = jnp.concatenate([*pieces, tail, jnp.zeros((rest, rows), F32)], axis=0)
    table_ref[...] = table.astype(BF16)
    wide = jnp.concatenate([jnp.broadcast_to(tail[k : k + 1], (MAIN, rows)) for k in range(experts)], axis=0)
    spread = dot(wide.astype(BF16), spread_ref[...])
    shape = (experts * MAIN, rows * chunks)
    tails_ref[...] = jnp.where(iota(shape, 0) % MAIN == iota(shape, 1) // rows, spread, 0.0).astype(BF16)
    weighed = [pieces[k] * gate[k : k + 1] for k in range(experts)]
    mixing = jnp.concatenate([*weighed, tail * gate, jnp.zeros((rest, rows), F32)], axis=0).T
    high, low = split_pair(mixing)
    mixing_ref[...] = jnp.concatenate([high, low], axis=0)


def chip_kernel(quarter, part_ref, near_ref, after_ref, chip_ref, sent_ref):
    del after_ref
    side = lax.axis_index("tensor") % 2
    for o in range(2):
        columns = strip(2 * o + side, quarter)
        total = part_ref[:, columns].astype(F32) + near_ref[:, columns].astype(F32)
        chip_ref[:, o * quarter : (o + 1) * quarter] = total
        sent_ref[:, o * quarter : (o + 1) * quarter] = total.astype(BF16)


def dispatch_kernel(quarter, experts, residual_ref, chip_ref, far_ref, gain_ref, table_ref, tails_ref, hidden_ref, *block_refs):
    tensor = lax.axis_index("tensor")
    side = tensor % 2
    rows = chip_ref.shape[0]
    squares = jnp.zeros((rows, 1), F32)
    gained = []
    for o in range(2):
        here = slice(o * quarter, (o + 1) * quarter)
        columns = strip(2 * o + side, quarter)
        hidden = residual_ref[:, columns] + chip_ref[:, here] + far_ref[:, here].astype(F32)
        squares = squares + jnp.sum(hidden * hidden, axis=1, keepdims=True)
        gained.append((hidden * gain_ref[:, columns]).astype(BF16))

        @pl.when(o == tensor // 2)
        def _():
            hidden_ref[...] = hidden

    table = table_ref[...]
    main = table[: experts * MAIN]
    lanes = jnp.sum(jnp.where(iota((rows, rows), 0) == iota((rows, rows), 1), squares, 0.0), axis=0, keepdims=True)
    high = lanes.astype(BF16).astype(F32)
    pick = iota((MAIN, rows), 0)
    pair = jnp.where(pick == 0, high, jnp.where(pick == 1, lanes - high, 0.0)).astype(BF16)
    slots = dot(pair, table, ((1,), (1,)))
    for o in range(2):
        picked = dot(main, gained[o]).astype(BF16)
        for k in range(experts):
            block_refs[k][:, o * quarter : (o + 1) * quarter] = picked[k * MAIN : (k + 1) * MAIN]
    parts = [g[:, i * LANES : (i + 1) * LANES] for g in gained for i in range(quarter // LANES)]
    tile = dot(tails_ref[...], jnp.concatenate(parts, axis=0))
    row = iota(tile.shape, 0) % MAIN
    tile = jnp.where(row == MAIN - 2, slots[0:1], jnp.where(row == MAIN - 1, slots[1:2], tile)).astype(BF16)
    for k in range(experts):
        block_refs[k][:, 2 * quarter :] = tile[k * MAIN : (k + 1) * MAIN]


def pack_kernel(experts, *refs):
    for ref, k in zip(refs, reversed(range(experts))):
        refs[-1][k * MAIN : (k + 1) * MAIN] = ref[...]


def unpack(tiles, chunks):
    tiles = [tile.astype(F32) for tile in tiles]
    row = iota((8, LANES), 0)
    parts = []
    for j in range(chunks):
        part = jnp.zeros((8, LANES), F32)
        for k, tile in enumerate(tiles):
            part = jnp.where(row == k, tile[j : j + 1], part)
        parts.append(jnp.concatenate([part, jnp.zeros((MAIN - 8, LANES), F32)], axis=0).astype(BF16))
    return parts


def pack(last, experts):
    row = iota((8, LANES), 0)
    tiles = []
    for k in range(experts):
        tile = jnp.zeros((8, LANES), F32)
        for j in range(last.shape[1] // LANES):
            tile = jnp.where(row == j, last[k : k + 1, j * LANES : (j + 1) * LANES], tile)
        tiles += [tile, jnp.zeros((MAIN - 8, LANES), F32)]
    return jnp.concatenate(tiles, axis=0)


def project(quarter, experts, ref, which, gate_ref, up_ref):
    tiles = [ref[k * MAIN : (k + 1) * MAIN, 2 * quarter :] for k in range(experts)]
    last = unpack(tiles, 2 * quarter // LANES)
    gated = upward = 0.0
    per = quarter // LANES
    for o in range(2):
        tails = jnp.concatenate(last[o * per : (o + 1) * per], axis=1)
        inputs = jnp.concatenate([ref[:, o * quarter : (o + 1) * quarter], tails], axis=0)
        here = strip(2 * o + which, quarter)
        gated = gated + dot(inputs, gate_ref[0, here, :])
        upward = upward + dot(inputs, up_ref[0, here, :])
    return gated, upward


def own_kernel(quarter, experts, own_ref, gate_ref, up_ref, gated_ref, upward_ref):
    side = lax.axis_index("tensor") % 2
    gated_ref[...], upward_ref[...] = project(quarter, experts, own_ref, side, gate_ref, up_ref)


def other_kernel(
    quarter, experts, own_ref, other_ref, gated_ref, upward_ref, gate_ref, up_ref, down_ref, active_ref, sent_ref
):
    side = lax.axis_index("tensor") % 2
    main, features = experts * MAIN, 4 * quarter
    lane = iota((1, LANES), 1)
    total = jnp.zeros((1, LANES), F32)
    for ref in (own_ref, other_ref):
        for k in range(experts):
            pair = ref[k * MAIN : (k + 1) * MAIN, 2 * quarter :].astype(F32)
            value = pair[MAIN - 2 : MAIN - 1] + pair[MAIN - 1 : MAIN]
            total = total + jnp.where((lane // MAIN == k) | (lane == main + k), value, 0.0)
    gated, upward = project(quarter, experts, other_ref, 1 - side, gate_ref, up_ref)
    gated, upward = gated + gated_ref[...], upward + upward_ref[...]
    shape = (gated.shape[0], LANES)
    column = jnp.sum(jnp.where(iota(shape, 0) == iota(shape, 1), total, 0.0), axis=1, keepdims=True)
    inverse = lax.rsqrt(column / features + EPSILON)
    gated, upward = gated * inverse, upward * inverse
    active = (gated / (1.0 + jnp.exp(-gated)) * upward).astype(BF16)
    active_ref[...] = active
    produce(quarter, active, down_ref, 1 - side, sent_ref)


def produce(quarter, active, down_ref, which, ref):
    for o in range(2):
        value = dot(active, down_ref[0, :, strip(2 * o + which, quarter)]).astype(BF16)
        ref[:, o * quarter : (o + 1) * quarter] = value[: ref.shape[0]]


def kept_kernel(quarter, active_ref, down_ref, kept_ref):
    produce(quarter, active_ref[...], down_ref, lax.axis_index("tensor") % 2, kept_ref)


def near_kernel(quarter, experts, kept_ref, near_ref, own_ref, far_ref, rest_ref):
    o = lax.axis_index("tensor") // 2
    main, rest = experts * MAIN, rest_ref.shape[0]

    def total(index):
        columns = strip(index, quarter)
        value = kept_ref[:, columns].astype(F32) + near_ref[:, columns].astype(F32)
        return value[:main], pack(value[main:], experts)

    value, tiles = total(1 - o)
    value, tiles = value.astype(BF16), tiles.astype(BF16)
    far_ref[:, :quarter], far_ref[:, quarter:] = value[rest:], tiles[rest:]
    rest_ref[:, :quarter], rest_ref[:, quarter:] = value[:rest], tiles[:rest]
    own_ref[:, :quarter], own_ref[:, quarter:] = total(o)


def far_kernel(start, own_ref, far_ref, *block_refs):
    for i, ref in enumerate(block_refs):
        here = slice(start + i * MAIN, start + (i + 1) * MAIN)
        ref[...] = (own_ref[here] + far_ref[i * MAIN : (i + 1) * MAIN].astype(F32)).astype(BF16)


def combine_kernel(experts, quarter, hidden_ref, mixing_ref, *refs):
    rows = hidden_ref.shape[0]
    blocks = [ref[...] for ref in refs[:experts]][::-1]
    last = jnp.concatenate(unpack([block[:, quarter:] for block in blocks], quarter // LANES), axis=1)
    slots = jnp.concatenate([*[block[:, :quarter] for block in blocks], last], axis=0)
    both = dot(mixing_ref[:, : slots.shape[0]], slots)
    refs[-1][...] = hidden_ref[...] + both[:rows] + both[rows:]


def local_kernels(residual, attention_part, norm_gain, expert_ids, gate_weights, w_gate, w_up, w_down):
    rows, features = residual.shape
    experts = lax.axis_size("expert")
    quarter = features // 4
    width = 2 * quarter
    chunks = width // LANES
    steps = range(1, experts)
    part = attention_part[0]
    near = xor_permute(part, "tensor", 1)
    before, spread = call(
        functools.partial(constant_kernel, rows), (out((rows, rows), BF16), out((rows, rows * chunks), BF16))
    )
    table, tails, mixing = call(
        functools.partial(table_kernel, experts, rows, chunks),
        (out((LANES, rows), BF16), out((experts * MAIN, rows * chunks), BF16), out((2 * rows, LANES), BF16)),
        before,
        spread,
        expert_ids.T,
        gate_weights.T,
    )
    chip, chip_sent = call(
        functools.partial(chip_kernel, quarter), (out((rows, width), F32), out((rows, width), BF16)), part, near, mixing
    )
    far = xor_permute(chip_sent, "tensor", 2)
    block = out((MAIN, width + LANES), BF16)
    hidden, *blocks = call(
        functools.partial(dispatch_kernel, quarter, experts),
        (out((rows, quarter), F32), *[block] * experts),
        residual,
        chip,
        far,
        norm_gain[None],
        table,
        tails,
    )
    arrived = [*[xor_permute(blocks[k], "expert", k) for k in reversed(steps)], blocks[0]]
    packed = out((experts * MAIN, width + LANES), BF16)
    (arrived,) = call(functools.partial(pack_kernel, experts), (packed,), *arrived, flops=0)
    other = xor_permute(arrived, "tensor", 1)
    main, slots = experts * MAIN, (experts + 1) * MAIN
    packed_width, used = quarter + LANES, main + 8
    hidden_count = w_gate.shape[2]
    sums = out((slots, hidden_count), F32)
    gated, upward = call(functools.partial(own_kernel, quarter, experts), (sums, sums), arrived, w_gate, w_up)
    active, sent = call(
        functools.partial(other_kernel, quarter, experts),
        (out((slots, hidden_count), BF16), out((used, width), BF16)),
        arrived,
        other,
        gated,
        upward,
        w_gate,
        w_up,
        w_down,
    )
    (kept,) = call(functools.partial(kept_kernel, quarter), (out((used, width), BF16),), active, w_down)
    near = xor_permute(sent, "tensor", 1)
    early = 2
    rest = main - early * MAIN
    own, far, others = call(
        functools.partial(near_kernel, quarter, experts),
        (out((main, packed_width), F32), out((main - rest, packed_width), BF16), out((rest, packed_width), BF16)),
        kept,
        near,
    )
    far, others = xor_permute(far, "tensor", 2), xor_permute(others, "tensor", 2)
    block = out((MAIN, packed_width), BF16)
    farthest = call(functools.partial(far_kernel, rest), [block] * early, own, far)
    blocks = [*call(functools.partial(far_kernel, 0), [block] * (experts - early), own, others), *farthest]
    blocks = [*[xor_permute(blocks[k], "expert", k) for k in reversed(steps)], blocks[0]]
    (result,) = call(
        functools.partial(combine_kernel, experts, quarter), (out((rows, quarter), F32),), hidden, mixing, *blocks
    )
    return result


def local(residual, *others):
    rows, features = residual.shape
    fits = lax.axis_size("tensor") == 4 and lax.axis_size("expert") == 4 and rows % 16 == 0 and rows <= LANES
    quarter = features // 4
    if fits and quarter % LANES == 0 and 2 * quarter // LANES <= MAIN - 2:
        return local_kernels(residual, *others)
    return local_general(residual, *others)


def local_general(residual, attention_part, norm_gain, expert_ids, gate_weights, w_gate, w_up, w_down):
    rows, features = residual.shape
    tensor_count = lax.axis_size("tensor")
    expert_count = lax.axis_size("expert")
    tensor = lax.axis_index("tensor")
    expert = lax.axis_index("expert")
    quarter = features // tensor_count
    outer = tensor_count // 2
    side = tensor % 2

    def strips(value):
        shaped = value.reshape(value.shape[0], outer, 2, quarter)
        return lax.dynamic_index_in_dim(shaped, side, 2, keepdims=False)

    part = attention_part[0]
    near = xor_permute(part, "tensor", 1)
    chip = strips(part.astype(jnp.float32) + near.astype(jnp.float32))
    chip_sent = chip.astype(jnp.bfloat16)
    far = [xor_permute(chip_sent, "tensor", 2 * step) for step in range(1, outer)]

    relative = expert_ids ^ expert
    blocks = jnp.arange(expert_count, dtype=jnp.int32)
    chosen = relative[:, :, None] == blocks[None, None, :]
    named = jnp.any(chosen, axis=1)
    gates = jnp.sum(jnp.where(chosen, gate_weights[:, :, None], 0.0), axis=1)
    below = jnp.arange(rows)[:, None] > jnp.arange(rows)[None, :]
    position = jnp.dot(below.astype(jnp.bfloat16), named.astype(jnp.bfloat16), preferred_element_type=jnp.float32)
    slots = jnp.arange(CAP, dtype=jnp.float32)
    table = (position.T[:, None, :] == slots[None, :, None]) & named.T[:, None, :]
    mixing = jnp.where(table, gates.T[:, None, :], 0.0).reshape(expert_count * CAP, rows)
    table = table.astype(jnp.bfloat16)

    hidden = strips(residual) + chip
    for value in far:
        hidden = hidden + value.astype(jnp.float32)
    squares = jnp.sum(hidden * hidden, axis=(1, 2))
    high, low = split_pair(squares)
    extra = jnp.zeros((rows, 128), jnp.bfloat16).at[:, 0].set(high).at[:, 1].set(low)
    gained = (hidden * strips(norm_gain[None])).astype(jnp.bfloat16).reshape(rows, outer * quarter)
    sent = jnp.concatenate([gained, extra], axis=1)
    arrived = []
    for step in range(expert_count):
        block = jnp.dot(table[step], sent, preferred_element_type=jnp.float32).astype(jnp.bfloat16)
        arrived.append(xor_permute(block, "expert", step) if step else block)
    other = [xor_permute(block, "tensor", 1) for block in arrived]
    arrived, other = jnp.concatenate(arrived, axis=0), jnp.concatenate(other, axis=0)

    def columns(value):
        return value[:, : outer * quarter].reshape(-1, outer, quarter)

    first = jnp.where(side == 0, arrived, other)
    second = jnp.where(side == 0, other, arrived)
    inputs = jnp.stack([columns(first), columns(second)], axis=2).reshape(-1, features)
    tails = (arrived[:, outer * quarter :].astype(jnp.float32), other[:, outer * quarter :].astype(jnp.float32))
    total = tails[0][:, 0] + tails[0][:, 1] + tails[1][:, 0] + tails[1][:, 1]
    inverse = lax.rsqrt(total / features + EPSILON)[:, None]
    gated = jnp.dot(inputs, w_gate[0], preferred_element_type=jnp.float32) * inverse
    upward = jnp.dot(inputs, w_up[0], preferred_element_type=jnp.float32) * inverse
    active = (jax.nn.silu(gated) * upward).astype(jnp.bfloat16)
    produced = jnp.dot(active, w_down[0], preferred_element_type=jnp.float32)

    def own_columns(index):
        return lax.dynamic_slice_in_dim(produced, index * quarter, quarter, 1)

    reduced = own_columns(tensor)
    for step in range(1, tensor_count):
        piece = own_columns(tensor ^ step).astype(jnp.bfloat16)
        reduced = reduced + xor_permute(piece, "tensor", step).astype(jnp.float32)
    reduced = reduced.astype(jnp.bfloat16).reshape(expert_count, CAP, quarter)
    returned = [xor_permute(reduced[k], "expert", k) if k else reduced[k] for k in range(expert_count)]
    returned = jnp.concatenate(returned, axis=0)
    high, low = split_pair(mixing)
    dims = (((0,), (0,)), ((), ()))
    combined = lax.dot_general(high, returned, dims, preferred_element_type=jnp.float32)
    combined = combined + lax.dot_general(low, returned, dims, preferred_element_type=jnp.float32)
    return lax.dynamic_index_in_dim(hidden, tensor // 2, 1, keepdims=False) + combined


def solution(mesh):
    in_specs = (
        P(("group", "expert"), None),
        P("tensor", ("group", "expert"), None),
        P(),
        P(("group", "expert"), None),
        P(("group", "expert"), None),
        P("expert", None, "tensor"),
        P("expert", None, "tensor"),
        P("expert", "tensor", None),
    )
    out_specs = P(("group", "expert"), "tensor")
    return jax.shard_map(local, mesh=mesh, in_specs=in_specs, out_specs=out_specs, check_vma=False)
```

```python
import functools

import jax
import jax.numpy as jnp
from jax import lax
from jax.experimental import pallas as pl
from jax.experimental.pallas import tpu as pltpu
from jax.sharding import PartitionSpec as P

CAP = 17
EPSILON = 1e-06
LANES = 128
MAIN = 16
FLOPS = 4 << 30
BF16, F32 = jnp.bfloat16, jnp.float32


def xor_permute(value, axis, step):
    count = lax.axis_size(axis)
    return lax.ppermute(value, axis, [(i, i ^ step) for i in range(count)])


def split_pair(value):
    high = value.astype(jnp.bfloat16)
    return high, (value - high.astype(jnp.float32)).astype(jnp.bfloat16)


def call(kernel, outs, *args, scratch=(), vmem=8 << 20, flops=FLOPS, name=None):
    vmem_spec = pl.BlockSpec(memory_space=pltpu.VMEM)
    moved = sum(a.size * a.dtype.itemsize for a in (*args, *outs))
    return pl.pallas_call(
        kernel,
        out_shape=tuple(outs),
        in_specs=[vmem_spec] * len(args),
        out_specs=(vmem_spec,) * len(outs),
        scratch_shapes=list(scratch),
        compiler_params=pltpu.CompilerParams(vmem_limit_bytes=vmem),
        cost_estimate=pl.CostEstimate(flops=flops, bytes_accessed=moved, transcendentals=0),
        name=name,
    )(*args)


def out(shape, dtype):
    return jax.ShapeDtypeStruct(shape, dtype)


def iota(shape, dim):
    return lax.broadcasted_iota(jnp.int32, shape, dim)


def onehot(mask):
    return jnp.where(mask, 1.0, 0.0)


def dot(left, right, contract=((1,), (0,))):
    return lax.dot_general(left, right, (contract, ((), ())), preferred_element_type=F32)


def strip(index, quarter):
    return pl.ds(pl.multiple_of(index * quarter, LANES), quarter)


def constant_kernel(rows, before_ref, spread_ref):
    before_ref[...] = onehot(iota((rows, rows), 0) < iota((rows, rows), 1)).astype(BF16)
    shape = spread_ref.shape
    spread_ref[...] = onehot(iota(shape, 0) == iota(shape, 1) % rows).astype(BF16)


def table_kernel(experts, rows, chunks, before_ref, spread_ref, ids_ref, gates_ref, table_ref, slots_ref, tails_ref, mixing_ref):
    expert = lax.axis_index("expert")
    relative = ids_ref[...] ^ expert
    gates = gates_ref[...]
    kinds = iota((8, rows), 0)
    named, gate = jnp.zeros((8, rows), jnp.bool_), jnp.zeros((8, rows), F32)
    for choice in range(relative.shape[0]):
        hit = relative[choice : choice + 1] == kinds
        named = named | hit
        gate = gate + jnp.where(hit, gates[choice : choice + 1], 0.0)
    position = dot(onehot(named).astype(BF16), before_ref[...])
    position = jnp.where(named, position, -1.0)
    slot = iota((MAIN, rows), 0).astype(F32)
    pieces = [onehot(position[k : k + 1] == slot) for k in range(experts)]
    tail = onehot(position == float(MAIN))
    rest = LANES - experts * MAIN - 8
    table = jnp.concatenate([*pieces, tail, jnp.zeros((rest, rows), F32)], axis=0)
    table_ref[...] = table[: experts * MAIN].astype(BF16)
    slots_ref[...] = table.T
    wide = jnp.concatenate([jnp.broadcast_to(tail[k : k + 1], (MAIN, rows)) for k in range(experts)], axis=0)
    spread = dot(wide.astype(BF16), spread_ref[...])
    shape = (experts * MAIN, rows * chunks)
    tails_ref[...] = jnp.where(iota(shape, 0) % MAIN == iota(shape, 1) // rows, spread, 0.0).astype(BF16)
    weighed = [pieces[k] * gate[k : k + 1] for k in range(experts)]
    mixing = jnp.concatenate([*weighed, tail * gate, jnp.zeros((rest, rows), F32)], axis=0).T
    high, low = split_pair(mixing)
    mixing_ref[...] = jnp.concatenate([high, low], axis=0)


def chip_kernel(quarter, part_ref, near_ref, after_ref, chip_ref, sent_ref):
    del after_ref
    side = lax.axis_index("tensor") % 2
    for o in range(2):
        columns = strip(2 * o + side, quarter)
        total = part_ref[:, columns].astype(F32) + near_ref[:, columns].astype(F32)
        chip_ref[:, o * quarter : (o + 1) * quarter] = total
        sent_ref[:, o * quarter : (o + 1) * quarter] = total.astype(BF16)


def dispatch_kernel(quarter, experts, residual_ref, chip_ref, far_ref, gain_ref, table_ref, slots_ref, tails_ref, hidden_ref, *block_refs):
    tensor = lax.axis_index("tensor")
    side = tensor % 2
    rows = chip_ref.shape[0]
    squares = jnp.zeros((rows, LANES), F32)
    gained = []
    for o in range(2):
        here = slice(o * quarter, (o + 1) * quarter)
        columns = strip(2 * o + side, quarter)
        hidden = residual_ref[:, columns] + chip_ref[:, here] + far_ref[:, here].astype(F32)
        for i in range(quarter // LANES):
            part = hidden[:, i * LANES : (i + 1) * LANES]
            squares = squares + part * part
        gained.append((hidden * gain_ref[:, columns]).astype(BF16))

        @pl.when(o == tensor // 2)
        def _():
            hidden_ref[...] = hidden

    squares = jnp.sum(slots_ref[...] * jnp.sum(squares, axis=1, keepdims=True), axis=0, keepdims=True)
    high = squares.astype(BF16).astype(F32)
    low = squares - high
    for o in range(2):
        picked = dot(table_ref[...], gained[o]).astype(BF16)
        for k in range(experts):
            block_refs[k][:, o * quarter : (o + 1) * quarter] = picked[k * MAIN : (k + 1) * MAIN]
    parts = [g[:, i * LANES : (i + 1) * LANES] for g in gained for i in range(quarter // LANES)]
    tile = dot(tails_ref[...], jnp.concatenate(parts, axis=0))
    row = iota(tile.shape, 0) % MAIN
    tile = jnp.where(row == MAIN - 2, high, jnp.where(row == MAIN - 1, low, tile)).astype(BF16)
    for k in range(experts):
        block_refs[k][:, 2 * quarter :] = tile[k * MAIN : (k + 1) * MAIN]


def pack_kernel(experts, *refs):
    for ref, k in zip(refs, reversed(range(experts))):
        refs[-1][k * MAIN : (k + 1) * MAIN] = ref[...]


def unpack(tiles, chunks):
    tiles = [tile.astype(F32) for tile in tiles]
    row = iota((8, LANES), 0)
    parts = []
    for j in range(chunks):
        part = jnp.zeros((8, LANES), F32)
        for k, tile in enumerate(tiles):
            part = jnp.where(row == k, tile[j : j + 1], part)
        parts.append(jnp.concatenate([part, jnp.zeros((MAIN - 8, LANES), F32)], axis=0).astype(BF16))
    return parts


def pack(last, experts):
    row = iota((8, LANES), 0)
    tiles = []
    for k in range(experts):
        tile = jnp.zeros((8, LANES), F32)
        for j in range(last.shape[1] // LANES):
            tile = jnp.where(row == j, last[k : k + 1, j * LANES : (j + 1) * LANES], tile)
        tiles += [tile, jnp.zeros((MAIN - 8, LANES), F32)]
    return jnp.concatenate(tiles, axis=0)


def project(quarter, experts, ref, which, gate_ref, up_ref):
    tiles = [ref[k * MAIN : (k + 1) * MAIN, 2 * quarter :] for k in range(experts)]
    last = unpack(tiles, 2 * quarter // LANES)
    gated = upward = 0.0
    per = quarter // LANES
    for o in range(2):
        tails = jnp.concatenate(last[o * per : (o + 1) * per], axis=1)
        inputs = jnp.concatenate([ref[:, o * quarter : (o + 1) * quarter], tails], axis=0)
        here = strip(2 * o + which, quarter)
        gated = gated + dot(inputs, gate_ref[0, here, :])
        upward = upward + dot(inputs, up_ref[0, here, :])
    return gated, upward


def own_kernel(quarter, experts, own_ref, gate_ref, up_ref, gated_ref, upward_ref):
    side = lax.axis_index("tensor") % 2
    gated_ref[...], upward_ref[...] = project(quarter, experts, own_ref, side, gate_ref, up_ref)


def other_kernel(
    quarter, experts, own_ref, other_ref, gated_ref, upward_ref, gate_ref, up_ref, down_ref, active_ref, sent_ref
):
    side = lax.axis_index("tensor") % 2
    main, features = experts * MAIN, 4 * quarter
    lane = iota((1, LANES), 1)
    total = jnp.zeros((1, LANES), F32)
    for ref in (own_ref, other_ref):
        for k in range(experts):
            pair = ref[k * MAIN : (k + 1) * MAIN, 2 * quarter :].astype(F32)
            value = pair[MAIN - 2 : MAIN - 1] + pair[MAIN - 1 : MAIN]
            total = total + jnp.where((lane // MAIN == k) | (lane == main + k), value, 0.0)
    gated, upward = project(quarter, experts, other_ref, 1 - side, gate_ref, up_ref)
    gated, upward = gated + gated_ref[...], upward + upward_ref[...]
    shape = (gated.shape[0], LANES)
    column = jnp.sum(jnp.where(iota(shape, 0) == iota(shape, 1), total, 0.0), axis=1, keepdims=True)
    inverse = lax.rsqrt(column / features + EPSILON)
    gated, upward = gated * inverse, upward * inverse
    active = (gated / (1.0 + jnp.exp(-gated)) * upward).astype(BF16)
    active_ref[...] = active
    produce(quarter, active, down_ref, 1 - side, sent_ref)


def produce(quarter, active, down_ref, which, ref):
    for o in range(2):
        value = dot(active, down_ref[0, :, strip(2 * o + which, quarter)]).astype(BF16)
        ref[:, o * quarter : (o + 1) * quarter] = value[: ref.shape[0]]


def kept_kernel(quarter, active_ref, down_ref, kept_ref):
    produce(quarter, active_ref[...], down_ref, lax.axis_index("tensor") % 2, kept_ref)


def near_kernel(quarter, experts, kept_ref, near_ref, own_ref, far_ref, rest_ref):
    o = lax.axis_index("tensor") // 2
    main, rest = experts * MAIN, rest_ref.shape[0]

    def total(index):
        columns = strip(index, quarter)
        value = kept_ref[:, columns].astype(F32) + near_ref[:, columns].astype(F32)
        return value[:main], pack(value[main:], experts)

    value, tiles = total(1 - o)
    value, tiles = value.astype(BF16), tiles.astype(BF16)
    far_ref[:, :quarter], far_ref[:, quarter:] = value[rest:], tiles[rest:]
    rest_ref[:, :quarter], rest_ref[:, quarter:] = value[:rest], tiles[:rest]
    own_ref[:, :quarter], own_ref[:, quarter:] = total(o)


def far_kernel(start, own_ref, far_ref, *block_refs):
    for i, ref in enumerate(block_refs):
        here = slice(start + i * MAIN, start + (i + 1) * MAIN)
        ref[...] = (own_ref[here] + far_ref[i * MAIN : (i + 1) * MAIN].astype(F32)).astype(BF16)


def combine_kernel(experts, quarter, hidden_ref, mixing_ref, *refs):
    rows = hidden_ref.shape[0]
    blocks = [ref[...] for ref in refs[:experts]][::-1]
    last = jnp.concatenate(unpack([block[:, quarter:] for block in blocks], quarter // LANES), axis=1)
    slots = jnp.concatenate([*[block[:, :quarter] for block in blocks], last], axis=0)
    both = dot(mixing_ref[:, : slots.shape[0]], slots)
    refs[-1][...] = hidden_ref[...] + both[:rows] + both[rows:]


def local_kernels(residual, attention_part, norm_gain, expert_ids, gate_weights, w_gate, w_up, w_down):
    rows, features = residual.shape
    experts = lax.axis_size("expert")
    quarter = features // 4
    width = 2 * quarter
    chunks = width // LANES
    steps = range(1, experts)
    part = attention_part[0]
    near = xor_permute(part, "tensor", 1)
    before, spread = call(
        functools.partial(constant_kernel, rows), (out((rows, rows), BF16), out((rows, rows * chunks), BF16))
    )
    table, slots, tails, mixing = call(
        functools.partial(table_kernel, experts, rows, chunks),
        (
            out((experts * MAIN, rows), BF16),
            out((rows, LANES), F32),
            out((experts * MAIN, rows * chunks), BF16),
            out((2 * rows, LANES), BF16),
        ),
        before,
        spread,
        expert_ids.T,
        gate_weights.T,
    )
    chip, chip_sent = call(
        functools.partial(chip_kernel, quarter), (out((rows, width), F32), out((rows, width), BF16)), part, near, mixing
    )
    far = xor_permute(chip_sent, "tensor", 2)
    block = out((MAIN, width + LANES), BF16)
    hidden, *blocks = call(
        functools.partial(dispatch_kernel, quarter, experts),
        (out((rows, quarter), F32), *[block] * experts),
        residual,
        chip,
        far,
        norm_gain[None],
        table,
        slots,
        tails,
    )
    arrived = [*[xor_permute(blocks[k], "expert", k) for k in reversed(steps)], blocks[0]]
    packed = out((experts * MAIN, width + LANES), BF16)
    (arrived,) = call(functools.partial(pack_kernel, experts), (packed,), *arrived, flops=0)
    other = xor_permute(arrived, "tensor", 1)
    main, slot_count = experts * MAIN, (experts + 1) * MAIN
    packed_width, used = quarter + LANES, main + 8
    hidden_count = w_gate.shape[2]
    sums = out((slot_count, hidden_count), F32)
    gated, upward = call(functools.partial(own_kernel, quarter, experts), (sums, sums), arrived, w_gate, w_up)
    active, sent = call(
        functools.partial(other_kernel, quarter, experts),
        (out((slot_count, hidden_count), BF16), out((used, width), BF16)),
        arrived,
        other,
        gated,
        upward,
        w_gate,
        w_up,
        w_down,
    )
    (kept,) = call(functools.partial(kept_kernel, quarter), (out((used, width), BF16),), active, w_down)
    near = xor_permute(sent, "tensor", 1)
    early = 2
    rest = main - early * MAIN
    own, far, others = call(
        functools.partial(near_kernel, quarter, experts),
        (out((main, packed_width), F32), out((main - rest, packed_width), BF16), out((rest, packed_width), BF16)),
        kept,
        near,
    )
    far, others = xor_permute(far, "tensor", 2), xor_permute(others, "tensor", 2)
    block = out((MAIN, packed_width), BF16)
    farthest = call(functools.partial(far_kernel, rest), [block] * early, own, far)
    blocks = [*call(functools.partial(far_kernel, 0), [block] * (experts - early), own, others), *farthest]
    blocks = [*[xor_permute(blocks[k], "expert", k) for k in reversed(steps)], blocks[0]]
    (result,) = call(
        functools.partial(combine_kernel, experts, quarter), (out((rows, quarter), F32),), hidden, mixing, *blocks
    )
    return result


def local(residual, *others):
    rows, features = residual.shape
    fits = lax.axis_size("tensor") == 4 and lax.axis_size("expert") == 4 and rows % 16 == 0 and rows <= LANES
    quarter = features // 4
    if fits and quarter % LANES == 0 and 2 * quarter // LANES <= MAIN - 2:
        return local_kernels(residual, *others)
    return local_general(residual, *others)


def local_general(residual, attention_part, norm_gain, expert_ids, gate_weights, w_gate, w_up, w_down):
    rows, features = residual.shape
    tensor_count = lax.axis_size("tensor")
    expert_count = lax.axis_size("expert")
    tensor = lax.axis_index("tensor")
    expert = lax.axis_index("expert")
    quarter = features // tensor_count
    outer = tensor_count // 2
    side = tensor % 2

    def strips(value):
        shaped = value.reshape(value.shape[0], outer, 2, quarter)
        return lax.dynamic_index_in_dim(shaped, side, 2, keepdims=False)

    part = attention_part[0]
    near = xor_permute(part, "tensor", 1)
    chip = strips(part.astype(jnp.float32) + near.astype(jnp.float32))
    chip_sent = chip.astype(jnp.bfloat16)
    far = [xor_permute(chip_sent, "tensor", 2 * step) for step in range(1, outer)]

    relative = expert_ids ^ expert
    blocks = jnp.arange(expert_count, dtype=jnp.int32)
    chosen = relative[:, :, None] == blocks[None, None, :]
    named = jnp.any(chosen, axis=1)
    gates = jnp.sum(jnp.where(chosen, gate_weights[:, :, None], 0.0), axis=1)
    below = jnp.arange(rows)[:, None] > jnp.arange(rows)[None, :]
    position = jnp.dot(below.astype(jnp.bfloat16), named.astype(jnp.bfloat16), preferred_element_type=jnp.float32)
    slots = jnp.arange(CAP, dtype=jnp.float32)
    table = (position.T[:, None, :] == slots[None, :, None]) & named.T[:, None, :]
    mixing = jnp.where(table, gates.T[:, None, :], 0.0).reshape(expert_count * CAP, rows)
    table = table.astype(jnp.bfloat16)

    hidden = strips(residual) + chip
    for value in far:
        hidden = hidden + value.astype(jnp.float32)
    squares = jnp.sum(hidden * hidden, axis=(1, 2))
    high, low = split_pair(squares)
    extra = jnp.zeros((rows, 128), jnp.bfloat16).at[:, 0].set(high).at[:, 1].set(low)
    gained = (hidden * strips(norm_gain[None])).astype(jnp.bfloat16).reshape(rows, outer * quarter)
    sent = jnp.concatenate([gained, extra], axis=1)
    arrived = []
    for step in range(expert_count):
        block = jnp.dot(table[step], sent, preferred_element_type=jnp.float32).astype(jnp.bfloat16)
        arrived.append(xor_permute(block, "expert", step) if step else block)
    other = [xor_permute(block, "tensor", 1) for block in arrived]
    arrived, other = jnp.concatenate(arrived, axis=0), jnp.concatenate(other, axis=0)

    def columns(value):
        return value[:, : outer * quarter].reshape(-1, outer, quarter)

    first = jnp.where(side == 0, arrived, other)
    second = jnp.where(side == 0, other, arrived)
    inputs = jnp.stack([columns(first), columns(second)], axis=2).reshape(-1, features)
    tails = (arrived[:, outer * quarter :].astype(jnp.float32), other[:, outer * quarter :].astype(jnp.float32))
    total = tails[0][:, 0] + tails[0][:, 1] + tails[1][:, 0] + tails[1][:, 1]
    inverse = lax.rsqrt(total / features + EPSILON)[:, None]
    gated = jnp.dot(inputs, w_gate[0], preferred_element_type=jnp.float32) * inverse
    upward = jnp.dot(inputs, w_up[0], preferred_element_type=jnp.float32) * inverse
    active = (jax.nn.silu(gated) * upward).astype(jnp.bfloat16)
    produced = jnp.dot(active, w_down[0], preferred_element_type=jnp.float32)

    def own_columns(index):
        return lax.dynamic_slice_in_dim(produced, index * quarter, quarter, 1)

    reduced = own_columns(tensor)
    for step in range(1, tensor_count):
        piece = own_columns(tensor ^ step).astype(jnp.bfloat16)
        reduced = reduced + xor_permute(piece, "tensor", step).astype(jnp.float32)
    reduced = reduced.astype(jnp.bfloat16).reshape(expert_count, CAP, quarter)
    returned = [xor_permute(reduced[k], "expert", k) if k else reduced[k] for k in range(expert_count)]
    returned = jnp.concatenate(returned, axis=0)
    high, low = split_pair(mixing)
    dims = (((0,), (0,)), ((), ()))
    combined = lax.dot_general(high, returned, dims, preferred_element_type=jnp.float32)
    combined = combined + lax.dot_general(low, returned, dims, preferred_element_type=jnp.float32)
    return lax.dynamic_index_in_dim(hidden, tensor // 2, 1, keepdims=False) + combined


def solution(mesh):
    in_specs = (
        P(("group", "expert"), None),
        P("tensor", ("group", "expert"), None),
        P(),
        P(("group", "expert"), None),
        P(("group", "expert"), None),
        P("expert", None, "tensor"),
        P("expert", None, "tensor"),
        P("expert", "tensor", None),
    )
    out_specs = P(("group", "expert"), "tensor")
    return jax.shard_map(local, mesh=mesh, in_specs=in_specs, out_specs=out_specs, check_vma=False)
```

```python
import functools

import jax
import jax.numpy as jnp
from jax import lax
from jax.experimental import pallas as pl
from jax.experimental.pallas import tpu as pltpu
from jax.sharding import PartitionSpec as P

CAP = 17
EPSILON = 1e-06
LANES = 128
MAIN = 16
FLOPS = 4 << 30
BF16, F32 = jnp.bfloat16, jnp.float32


def xor_permute(value, axis, step):
    count = lax.axis_size(axis)
    return lax.ppermute(value, axis, [(i, i ^ step) for i in range(count)])


def split_pair(value):
    high = value.astype(jnp.bfloat16)
    return high, (value - high.astype(jnp.float32)).astype(jnp.bfloat16)


def call(kernel, outs, *args, scratch=(), vmem=8 << 20, flops=FLOPS, name=None):
    vmem_spec = pl.BlockSpec(memory_space=pltpu.VMEM)
    moved = sum(a.size * a.dtype.itemsize for a in (*args, *outs))
    return pl.pallas_call(
        kernel,
        out_shape=tuple(outs),
        in_specs=[vmem_spec] * len(args),
        out_specs=(vmem_spec,) * len(outs),
        scratch_shapes=list(scratch),
        compiler_params=pltpu.CompilerParams(vmem_limit_bytes=vmem),
        cost_estimate=pl.CostEstimate(flops=flops, bytes_accessed=moved, transcendentals=0),
        name=name,
    )(*args)


def out(shape, dtype):
    return jax.ShapeDtypeStruct(shape, dtype)


def iota(shape, dim):
    return lax.broadcasted_iota(jnp.int32, shape, dim)


def onehot(mask):
    return jnp.where(mask, 1.0, 0.0)


def dot(left, right, contract=((1,), (0,))):
    return lax.dot_general(left, right, (contract, ((), ())), preferred_element_type=F32)


def strip(index, quarter):
    return pl.ds(pl.multiple_of(index * quarter, LANES), quarter)


def constant_kernel(rows, before_ref, spread_ref):
    before_ref[...] = onehot(iota((rows, rows), 0) < iota((rows, rows), 1)).astype(BF16)
    shape = spread_ref.shape
    spread_ref[...] = onehot(iota(shape, 0) == iota(shape, 1) % rows).astype(BF16)


def table_kernel(experts, rows, chunks, before_ref, spread_ref, ids_ref, gates_ref, table_ref, slots_ref, tails_ref, mixing_ref):
    expert = lax.axis_index("expert")
    relative = ids_ref[...] ^ expert
    gates = gates_ref[...]
    kinds = iota((8, rows), 0)
    named, gate = jnp.zeros((8, rows), jnp.bool_), jnp.zeros((8, rows), F32)
    for choice in range(relative.shape[0]):
        hit = relative[choice : choice + 1] == kinds
        named = named | hit
        gate = gate + jnp.where(hit, gates[choice : choice + 1], 0.0)
    position = dot(onehot(named).astype(BF16), before_ref[...])
    position = jnp.where(named, position, -1.0)
    slot = iota((MAIN, rows), 0).astype(F32)
    pieces = [onehot(position[k : k + 1] == slot) for k in range(experts)]
    tail = onehot(position == float(MAIN))
    rest = LANES - experts * MAIN - 8
    table = jnp.concatenate([*pieces, tail, jnp.zeros((rest, rows), F32)], axis=0)
    table_ref[...] = table[: experts * MAIN].astype(BF16)
    slots_ref[...] = table.T
    wide = jnp.concatenate([jnp.broadcast_to(tail[k : k + 1], (MAIN, rows)) for k in range(experts)], axis=0)
    spread = dot(wide.astype(BF16), spread_ref[...])
    shape = (experts * MAIN, rows * chunks)
    tails_ref[...] = jnp.where(iota(shape, 0) % MAIN == iota(shape, 1) // rows, spread, 0.0).astype(BF16)
    weighed = [pieces[k] * gate[k : k + 1] for k in range(experts)]
    mixing = jnp.concatenate([*weighed, tail * gate, jnp.zeros((rest, rows), F32)], axis=0).T
    high, low = split_pair(mixing)
    mixing_ref[...] = jnp.concatenate([high, low], axis=0)


def chip_kernel(quarter, part_ref, near_ref, after_ref, chip_ref, sent_ref):
    del after_ref
    side = lax.axis_index("tensor") % 2
    for o in range(2):
        columns = strip(2 * o + side, quarter)
        total = part_ref[:, columns].astype(F32) + near_ref[:, columns].astype(F32)
        chip_ref[:, o * quarter : (o + 1) * quarter] = total
        sent_ref[:, o * quarter : (o + 1) * quarter] = total.astype(BF16)


def dispatch_kernel(quarter, experts, residual_ref, chip_ref, far_ref, gain_ref, table_ref, slots_ref, tails_ref, hidden_ref, *block_refs):
    tensor = lax.axis_index("tensor")
    side = tensor % 2
    rows = chip_ref.shape[0]
    squares = jnp.zeros((rows, LANES), F32)
    gained = []
    for o in range(2):
        here = slice(o * quarter, (o + 1) * quarter)
        columns = strip(2 * o + side, quarter)
        hidden = residual_ref[:, columns] + chip_ref[:, here] + far_ref[:, here].astype(F32)
        for i in range(quarter // LANES):
            part = hidden[:, i * LANES : (i + 1) * LANES]
            squares = squares + part * part
        gained.append((hidden * gain_ref[:, columns]).astype(BF16))

        @pl.when(o == tensor // 2)
        def _():
            hidden_ref[...] = hidden

    squares = jnp.sum(slots_ref[...] * jnp.sum(squares, axis=1, keepdims=True), axis=0, keepdims=True)
    high = squares.astype(BF16).astype(F32)
    low = squares - high
    for o in range(2):
        picked = dot(table_ref[...], gained[o]).astype(BF16)
        for k in range(experts):
            block_refs[k][:, o * quarter : (o + 1) * quarter] = picked[k * MAIN : (k + 1) * MAIN]
    parts = [g[:, i * LANES : (i + 1) * LANES] for g in gained for i in range(quarter // LANES)]
    tile = dot(tails_ref[...], jnp.concatenate(parts, axis=0))
    row = iota(tile.shape, 0) % MAIN
    tile = jnp.where(row == MAIN - 2, high, jnp.where(row == MAIN - 1, low, tile)).astype(BF16)
    for k in range(experts):
        block_refs[k][:, 2 * quarter :] = tile[k * MAIN : (k + 1) * MAIN]


def pack_kernel(order, *refs):
    for ref, k in zip(refs, order):
        refs[-1][k * MAIN : (k + 1) * MAIN] = ref[...]


def unpack(tiles, chunks):
    tiles = [tile.astype(F32) for tile in tiles]
    row = iota((8, LANES), 0)
    parts = []
    for j in range(chunks):
        part = jnp.zeros((8, LANES), F32)
        for k, tile in enumerate(tiles):
            part = jnp.where(row == k, tile[j : j + 1], part)
        parts.append(jnp.concatenate([part, jnp.zeros((MAIN - 8, LANES), F32)], axis=0).astype(BF16))
    return parts


def pack(last, experts):
    row = iota((8, LANES), 0)
    tiles = []
    for k in range(experts):
        tile = jnp.zeros((8, LANES), F32)
        for j in range(last.shape[1] // LANES):
            tile = jnp.where(row == j, last[k : k + 1, j * LANES : (j + 1) * LANES], tile)
        tiles += [tile, jnp.zeros((MAIN - 8, LANES), F32)]
    return jnp.concatenate(tiles, axis=0)


def project(quarter, experts, ref, which, gate_ref, up_ref):
    tiles = [ref[k * MAIN : (k + 1) * MAIN, 2 * quarter :] for k in range(experts)]
    last = unpack(tiles, 2 * quarter // LANES)
    gated = upward = 0.0
    per = quarter // LANES
    for o in range(2):
        tails = jnp.concatenate(last[o * per : (o + 1) * per], axis=1)
        inputs = jnp.concatenate([ref[:, o * quarter : (o + 1) * quarter], tails], axis=0)
        here = strip(2 * o + which, quarter)
        gated = gated + dot(inputs, gate_ref[0, here, :])
        upward = upward + dot(inputs, up_ref[0, here, :])
    return gated, upward


def own_kernel(quarter, experts, own_ref, gate_ref, up_ref, gated_ref, upward_ref):
    side = lax.axis_index("tensor") % 2
    gated_ref[...], upward_ref[...] = project(quarter, experts, own_ref, side, gate_ref, up_ref)


def other_kernel(
    quarter, experts, own_ref, other_ref, gated_ref, upward_ref, gate_ref, up_ref, down_ref, active_ref, sent_ref
):
    side = lax.axis_index("tensor") % 2
    main, features = experts * MAIN, 4 * quarter
    lane = iota((1, LANES), 1)
    total = jnp.zeros((1, LANES), F32)
    for ref in (own_ref, other_ref):
        for k in range(experts):
            pair = ref[k * MAIN : (k + 1) * MAIN, 2 * quarter :].astype(F32)
            value = pair[MAIN - 2 : MAIN - 1] + pair[MAIN - 1 : MAIN]
            total = total + jnp.where((lane // MAIN == k) | (lane == main + k), value, 0.0)
    gated, upward = project(quarter, experts, other_ref, 1 - side, gate_ref, up_ref)
    gated, upward = gated + gated_ref[...], upward + upward_ref[...]
    shape = (gated.shape[0], LANES)
    column = jnp.sum(jnp.where(iota(shape, 0) == iota(shape, 1), total, 0.0), axis=1, keepdims=True)
    inverse = lax.rsqrt(column / features + EPSILON)
    gated, upward = gated * inverse, upward * inverse
    active = (gated / (1.0 + jnp.exp(-gated)) * upward).astype(BF16)
    active_ref[...] = active
    produce(quarter, active, down_ref, 1 - side, sent_ref)


def produce(quarter, active, down_ref, which, ref):
    for o in range(2):
        value = dot(active, down_ref[0, :, strip(2 * o + which, quarter)]).astype(BF16)
        ref[:, o * quarter : (o + 1) * quarter] = value[: ref.shape[0]]


def kept_kernel(quarter, active_ref, down_ref, kept_ref):
    produce(quarter, active_ref[...], down_ref, lax.axis_index("tensor") % 2, kept_ref)


def near_kernel(quarter, experts, kept_ref, near_ref, own_ref, far_ref, rest_ref):
    o = lax.axis_index("tensor") // 2
    main, rest = experts * MAIN, rest_ref.shape[0]

    def total(index):
        columns = strip(index, quarter)
        value = kept_ref[:, columns].astype(F32) + near_ref[:, columns].astype(F32)
        return value[:main], pack(value[main:], experts)

    value, tiles = total(1 - o)
    value, tiles = value.astype(BF16), tiles.astype(BF16)
    far_ref[:, :quarter], far_ref[:, quarter:] = value[rest:], tiles[rest:]
    rest_ref[:, :quarter], rest_ref[:, quarter:] = value[:rest], tiles[:rest]
    own_ref[:, :quarter], own_ref[:, quarter:] = total(o)


def far_kernel(start, own_ref, far_ref, *block_refs):
    for i, ref in enumerate(block_refs):
        here = slice(start + i * MAIN, start + (i + 1) * MAIN)
        ref[...] = (own_ref[here] + far_ref[i * MAIN : (i + 1) * MAIN].astype(F32)).astype(BF16)


def combine_kernel(order, quarter, hidden_ref, mixing_ref, *refs):
    rows = hidden_ref.shape[0]
    blocks = [refs[order.index(k)][...] for k in range(len(order))]
    last = jnp.concatenate(unpack([block[:, quarter:] for block in blocks], quarter // LANES), axis=1)
    slots = jnp.concatenate([*[block[:, :quarter] for block in blocks], last], axis=0)
    both = dot(mixing_ref[:, : slots.shape[0]], slots)
    refs[-1][...] = hidden_ref[...] + both[:rows] + both[rows:]


def local_kernels(residual, attention_part, norm_gain, expert_ids, gate_weights, w_gate, w_up, w_down):
    rows, features = residual.shape
    experts = lax.axis_size("expert")
    quarter = features // 4
    width = 2 * quarter
    chunks = width // LANES
    out_order, back_order = (2, 3, 1, 0), (3, 1, 2, 0)
    part = attention_part[0]
    near = xor_permute(part, "tensor", 1)
    before, spread = call(
        functools.partial(constant_kernel, rows), (out((rows, rows), BF16), out((rows, rows * chunks), BF16))
    )
    table, slots, tails, mixing = call(
        functools.partial(table_kernel, experts, rows, chunks),
        (
            out((experts * MAIN, rows), BF16),
            out((rows, LANES), F32),
            out((experts * MAIN, rows * chunks), BF16),
            out((2 * rows, LANES), BF16),
        ),
        before,
        spread,
        expert_ids.T,
        gate_weights.T,
    )
    chip, chip_sent = call(
        functools.partial(chip_kernel, quarter), (out((rows, width), F32), out((rows, width), BF16)), part, near, mixing
    )
    far = xor_permute(chip_sent, "tensor", 2)
    block = out((MAIN, width + LANES), BF16)
    hidden, *blocks = call(
        functools.partial(dispatch_kernel, quarter, experts),
        (out((rows, quarter), F32), *[block] * experts),
        residual,
        chip,
        far,
        norm_gain[None],
        table,
        slots,
        tails,
    )
    arrived = [*[xor_permute(blocks[k], "expert", k) for k in out_order[:-1]], blocks[0]]
    packed = out((experts * MAIN, width + LANES), BF16)
    (arrived,) = call(functools.partial(pack_kernel, out_order), (packed,), *arrived, flops=0)
    other = xor_permute(arrived, "tensor", 1)
    main, slot_count = experts * MAIN, (experts + 1) * MAIN
    packed_width, used = quarter + LANES, main + 8
    hidden_count = w_gate.shape[2]
    sums = out((slot_count, hidden_count), F32)
    gated, upward = call(functools.partial(own_kernel, quarter, experts), (sums, sums), arrived, w_gate, w_up)
    active, sent = call(
        functools.partial(other_kernel, quarter, experts),
        (out((slot_count, hidden_count), BF16), out((used, width), BF16)),
        arrived,
        other,
        gated,
        upward,
        w_gate,
        w_up,
        w_down,
    )
    (kept,) = call(functools.partial(kept_kernel, quarter), (out((used, width), BF16),), active, w_down)
    near = xor_permute(sent, "tensor", 1)
    early = 2
    rest = main - early * MAIN
    own, far, others = call(
        functools.partial(near_kernel, quarter, experts),
        (out((main, packed_width), F32), out((main - rest, packed_width), BF16), out((rest, packed_width), BF16)),
        kept,
        near,
    )
    far, others = xor_permute(far, "tensor", 2), xor_permute(others, "tensor", 2)
    block = out((MAIN, packed_width), BF16)
    farthest = call(functools.partial(far_kernel, rest), [block] * early, own, far)
    blocks = [*call(functools.partial(far_kernel, 0), [block] * (experts - early), own, others), *farthest]
    blocks = [*[xor_permute(blocks[k], "expert", k) for k in back_order[:-1]], blocks[0]]
    (result,) = call(
        functools.partial(combine_kernel, back_order, quarter), (out((rows, quarter), F32),), hidden, mixing, *blocks
    )
    return result


def local(residual, *others):
    rows, features = residual.shape
    fits = lax.axis_size("tensor") == 4 and lax.axis_size("expert") == 4 and rows % 16 == 0 and rows <= LANES
    quarter = features // 4
    if fits and quarter % LANES == 0 and 2 * quarter // LANES <= MAIN - 2:
        return local_kernels(residual, *others)
    return local_general(residual, *others)


def local_general(residual, attention_part, norm_gain, expert_ids, gate_weights, w_gate, w_up, w_down):
    rows, features = residual.shape
    tensor_count = lax.axis_size("tensor")
    expert_count = lax.axis_size("expert")
    tensor = lax.axis_index("tensor")
    expert = lax.axis_index("expert")
    quarter = features // tensor_count
    outer = tensor_count // 2
    side = tensor % 2

    def strips(value):
        shaped = value.reshape(value.shape[0], outer, 2, quarter)
        return lax.dynamic_index_in_dim(shaped, side, 2, keepdims=False)

    part = attention_part[0]
    near = xor_permute(part, "tensor", 1)
    chip = strips(part.astype(jnp.float32) + near.astype(jnp.float32))
    chip_sent = chip.astype(jnp.bfloat16)
    far = [xor_permute(chip_sent, "tensor", 2 * step) for step in range(1, outer)]

    relative = expert_ids ^ expert
    blocks = jnp.arange(expert_count, dtype=jnp.int32)
    chosen = relative[:, :, None] == blocks[None, None, :]
    named = jnp.any(chosen, axis=1)
    gates = jnp.sum(jnp.where(chosen, gate_weights[:, :, None], 0.0), axis=1)
    below = jnp.arange(rows)[:, None] > jnp.arange(rows)[None, :]
    position = jnp.dot(below.astype(jnp.bfloat16), named.astype(jnp.bfloat16), preferred_element_type=jnp.float32)
    slots = jnp.arange(CAP, dtype=jnp.float32)
    table = (position.T[:, None, :] == slots[None, :, None]) & named.T[:, None, :]
    mixing = jnp.where(table, gates.T[:, None, :], 0.0).reshape(expert_count * CAP, rows)
    table = table.astype(jnp.bfloat16)

    hidden = strips(residual) + chip
    for value in far:
        hidden = hidden + value.astype(jnp.float32)
    squares = jnp.sum(hidden * hidden, axis=(1, 2))
    high, low = split_pair(squares)
    extra = jnp.zeros((rows, 128), jnp.bfloat16).at[:, 0].set(high).at[:, 1].set(low)
    gained = (hidden * strips(norm_gain[None])).astype(jnp.bfloat16).reshape(rows, outer * quarter)
    sent = jnp.concatenate([gained, extra], axis=1)
    arrived = []
    for step in range(expert_count):
        block = jnp.dot(table[step], sent, preferred_element_type=jnp.float32).astype(jnp.bfloat16)
        arrived.append(xor_permute(block, "expert", step) if step else block)
    other = [xor_permute(block, "tensor", 1) for block in arrived]
    arrived, other = jnp.concatenate(arrived, axis=0), jnp.concatenate(other, axis=0)

    def columns(value):
        return value[:, : outer * quarter].reshape(-1, outer, quarter)

    first = jnp.where(side == 0, arrived, other)
    second = jnp.where(side == 0, other, arrived)
    inputs = jnp.stack([columns(first), columns(second)], axis=2).reshape(-1, features)
    tails = (arrived[:, outer * quarter :].astype(jnp.float32), other[:, outer * quarter :].astype(jnp.float32))
    total = tails[0][:, 0] + tails[0][:, 1] + tails[1][:, 0] + tails[1][:, 1]
    inverse = lax.rsqrt(total / features + EPSILON)[:, None]
    gated = jnp.dot(inputs, w_gate[0], preferred_element_type=jnp.float32) * inverse
    upward = jnp.dot(inputs, w_up[0], preferred_element_type=jnp.float32) * inverse
    active = (jax.nn.silu(gated) * upward).astype(jnp.bfloat16)
    produced = jnp.dot(active, w_down[0], preferred_element_type=jnp.float32)

    def own_columns(index):
        return lax.dynamic_slice_in_dim(produced, index * quarter, quarter, 1)

    reduced = own_columns(tensor)
    for step in range(1, tensor_count):
        piece = own_columns(tensor ^ step).astype(jnp.bfloat16)
        reduced = reduced + xor_permute(piece, "tensor", step).astype(jnp.float32)
    reduced = reduced.astype(jnp.bfloat16).reshape(expert_count, CAP, quarter)
    returned = [xor_permute(reduced[k], "expert", k) if k else reduced[k] for k in range(expert_count)]
    returned = jnp.concatenate(returned, axis=0)
    high, low = split_pair(mixing)
    dims = (((0,), (0,)), ((), ()))
    combined = lax.dot_general(high, returned, dims, preferred_element_type=jnp.float32)
    combined = combined + lax.dot_general(low, returned, dims, preferred_element_type=jnp.float32)
    return lax.dynamic_index_in_dim(hidden, tensor // 2, 1, keepdims=False) + combined


def solution(mesh):
    in_specs = (
        P(("group", "expert"), None),
        P("tensor", ("group", "expert"), None),
        P(),
        P(("group", "expert"), None),
        P(("group", "expert"), None),
        P("expert", None, "tensor"),
        P("expert", None, "tensor"),
        P("expert", "tensor", None),
    )
    out_specs = P(("group", "expert"), "tensor")
    return jax.shard_map(local, mesh=mesh, in_specs=in_specs, out_specs=out_specs, check_vma=False)
```

```python
import functools

import jax
import jax.numpy as jnp
from jax import lax
from jax.experimental import pallas as pl
from jax.experimental.pallas import tpu as pltpu
from jax.sharding import PartitionSpec as P

CAP = 17
EPSILON = 1e-06
LANES = 128
MAIN = 16
FLOPS = 4 << 30
BF16, F32 = jnp.bfloat16, jnp.float32


def xor_permute(value, axis, step):
    count = lax.axis_size(axis)
    return lax.ppermute(value, axis, [(i, i ^ step) for i in range(count)])


def cross_permute(value, step):
    experts, tensors = lax.axis_size("expert"), lax.axis_size("tensor")
    pairs = [(e * tensors + t, (e ^ step) * tensors + (t ^ 1)) for e in range(experts) for t in range(tensors)]
    return lax.ppermute(value, ("expert", "tensor"), pairs)


def split_pair(value):
    high = value.astype(jnp.bfloat16)
    return high, (value - high.astype(jnp.float32)).astype(jnp.bfloat16)


def call(kernel, outs, *args, scratch=(), vmem=8 << 20, flops=FLOPS, name=None):
    vmem_spec = pl.BlockSpec(memory_space=pltpu.VMEM)
    moved = sum(a.size * a.dtype.itemsize for a in (*args, *outs))
    return pl.pallas_call(
        kernel,
        out_shape=tuple(outs),
        in_specs=[vmem_spec] * len(args),
        out_specs=(vmem_spec,) * len(outs),
        scratch_shapes=list(scratch),
        compiler_params=pltpu.CompilerParams(vmem_limit_bytes=vmem),
        cost_estimate=pl.CostEstimate(flops=flops, bytes_accessed=moved, transcendentals=0),
        name=name,
    )(*args)


def out(shape, dtype):
    return jax.ShapeDtypeStruct(shape, dtype)


def iota(shape, dim):
    return lax.broadcasted_iota(jnp.int32, shape, dim)


def onehot(mask):
    return jnp.where(mask, 1.0, 0.0)


def dot(left, right, contract=((1,), (0,))):
    return lax.dot_general(left, right, (contract, ((), ())), preferred_element_type=F32)


def strip(index, quarter):
    return pl.ds(pl.multiple_of(index * quarter, LANES), quarter)


def constant_kernel(rows, before_ref, spread_ref):
    before_ref[...] = onehot(iota((rows, rows), 0) < iota((rows, rows), 1)).astype(BF16)
    shape = spread_ref.shape
    spread_ref[...] = onehot(iota(shape, 0) == iota(shape, 1) % rows).astype(BF16)


def table_kernel(experts, rows, chunks, before_ref, spread_ref, ids_ref, gates_ref, table_ref, slots_ref, tails_ref, mixing_ref):
    expert = lax.axis_index("expert")
    relative = ids_ref[...] ^ expert
    gates = gates_ref[...]
    kinds = iota((8, rows), 0)
    named, gate = jnp.zeros((8, rows), jnp.bool_), jnp.zeros((8, rows), F32)
    for choice in range(relative.shape[0]):
        hit = relative[choice : choice + 1] == kinds
        named = named | hit
        gate = gate + jnp.where(hit, gates[choice : choice + 1], 0.0)
    position = dot(onehot(named).astype(BF16), before_ref[...])
    position = jnp.where(named, position, -1.0)
    slot = iota((MAIN, rows), 0).astype(F32)
    pieces = [onehot(position[k : k + 1] == slot) for k in range(experts)]
    tail = onehot(position == float(MAIN))
    rest = LANES - experts * MAIN - 8
    table = jnp.concatenate([*pieces, tail, jnp.zeros((rest, rows), F32)], axis=0)
    table_ref[...] = table[: experts * MAIN].astype(BF16)
    slots_ref[...] = table.T
    wide = jnp.concatenate([jnp.broadcast_to(tail[k : k + 1], (MAIN, rows)) for k in range(experts)], axis=0)
    spread = dot(wide.astype(BF16), spread_ref[...])
    shape = (experts * MAIN, rows * chunks)
    tails_ref[...] = jnp.where(iota(shape, 0) % MAIN == iota(shape, 1) // rows, spread, 0.0).astype(BF16)
    weighed = [pieces[k] * gate[k : k + 1] for k in range(experts)]
    mixing = jnp.concatenate([*weighed, tail * gate, jnp.zeros((rest, rows), F32)], axis=0).T
    high, low = split_pair(mixing)
    mixing_ref[...] = jnp.concatenate([high, low], axis=0)


def chip_kernel(quarter, part_ref, near_ref, after_ref, chip_ref, sent_ref):
    del after_ref
    side = lax.axis_index("tensor") % 2
    for o in range(2):
        columns = strip(2 * o + side, quarter)
        total = part_ref[:, columns].astype(F32) + near_ref[:, columns].astype(F32)
        chip_ref[:, o * quarter : (o + 1) * quarter] = total
        sent_ref[:, o * quarter : (o + 1) * quarter] = total.astype(BF16)


def dispatch_kernel(quarter, experts, residual_ref, chip_ref, far_ref, gain_ref, table_ref, slots_ref, tails_ref, hidden_ref, *block_refs):
    tensor = lax.axis_index("tensor")
    side = tensor % 2
    rows = chip_ref.shape[0]
    squares = jnp.zeros((rows, LANES), F32)
    gained = []
    for o in range(2):
        here = slice(o * quarter, (o + 1) * quarter)
        columns = strip(2 * o + side, quarter)
        hidden = residual_ref[:, columns] + chip_ref[:, here] + far_ref[:, here].astype(F32)
        for i in range(quarter // LANES):
            part = hidden[:, i * LANES : (i + 1) * LANES]
            squares = squares + part * part
        gained.append((hidden * gain_ref[:, columns]).astype(BF16))

        @pl.when(o == tensor // 2)
        def _():
            hidden_ref[...] = hidden

    squares = jnp.sum(slots_ref[...] * jnp.sum(squares, axis=1, keepdims=True), axis=0, keepdims=True)
    high = squares.astype(BF16).astype(F32)
    low = squares - high
    for o in range(2):
        picked = dot(table_ref[...], gained[o]).astype(BF16)
        for k in range(experts):
            block_refs[k][:, o * quarter : (o + 1) * quarter] = picked[k * MAIN : (k + 1) * MAIN]
    parts = [g[:, i * LANES : (i + 1) * LANES] for g in gained for i in range(quarter // LANES)]
    tile = dot(tails_ref[...], jnp.concatenate(parts, axis=0))
    row = iota(tile.shape, 0) % MAIN
    tile = jnp.where(row == MAIN - 2, high, jnp.where(row == MAIN - 1, low, tile)).astype(BF16)
    for k in range(experts):
        block_refs[k][:, 2 * quarter :] = tile[k * MAIN : (k + 1) * MAIN]


def pack_kernel(experts, *refs):
    for ref, k in zip(refs, reversed(range(experts))):
        refs[-1][k * MAIN : (k + 1) * MAIN] = ref[...]


def unpack(tiles, chunks):
    tiles = [tile.astype(F32) for tile in tiles]
    row = iota((8, LANES), 0)
    parts = []
    for j in range(chunks):
        part = jnp.zeros((8, LANES), F32)
        for k, tile in enumerate(tiles):
            part = jnp.where(row == k, tile[j : j + 1], part)
        parts.append(jnp.concatenate([part, jnp.zeros((MAIN - 8, LANES), F32)], axis=0).astype(BF16))
    return parts


def pack(last, experts):
    row = iota((8, LANES), 0)
    tiles = []
    for k in range(experts):
        tile = jnp.zeros((8, LANES), F32)
        for j in range(last.shape[1] // LANES):
            tile = jnp.where(row == j, last[k : k + 1, j * LANES : (j + 1) * LANES], tile)
        tiles += [tile, jnp.zeros((MAIN - 8, LANES), F32)]
    return jnp.concatenate(tiles, axis=0)


def project(quarter, experts, ref, which, gate_ref, up_ref):
    tiles = [ref[k * MAIN : (k + 1) * MAIN, 2 * quarter :] for k in range(experts)]
    last = unpack(tiles, 2 * quarter // LANES)
    gated = upward = 0.0
    per = quarter // LANES
    for o in range(2):
        tails = jnp.concatenate(last[o * per : (o + 1) * per], axis=1)
        inputs = jnp.concatenate([ref[:, o * quarter : (o + 1) * quarter], tails], axis=0)
        here = strip(2 * o + which, quarter)
        gated = gated + dot(inputs, gate_ref[0, here, :])
        upward = upward + dot(inputs, up_ref[0, here, :])
    return gated, upward


def own_kernel(quarter, experts, own_ref, gate_ref, up_ref, gated_ref, upward_ref):
    side = lax.axis_index("tensor") % 2
    gated_ref[...], upward_ref[...] = project(quarter, experts, own_ref, side, gate_ref, up_ref)


def other_kernel(
    quarter, experts, own_ref, other_ref, gated_ref, upward_ref, gate_ref, up_ref, down_ref, active_ref, sent_ref
):
    side = lax.axis_index("tensor") % 2
    main, features = experts * MAIN, 4 * quarter
    lane = iota((1, LANES), 1)
    total = jnp.zeros((1, LANES), F32)
    for ref in (own_ref, other_ref):
        for k in range(experts):
            pair = ref[k * MAIN : (k + 1) * MAIN, 2 * quarter :].astype(F32)
            value = pair[MAIN - 2 : MAIN - 1] + pair[MAIN - 1 : MAIN]
            total = total + jnp.where((lane // MAIN == k) | (lane == main + k), value, 0.0)
    gated, upward = project(quarter, experts, other_ref, 1 - side, gate_ref, up_ref)
    gated, upward = gated + gated_ref[...], upward + upward_ref[...]
    shape = (gated.shape[0], LANES)
    column = jnp.sum(jnp.where(iota(shape, 0) == iota(shape, 1), total, 0.0), axis=1, keepdims=True)
    inverse = lax.rsqrt(column / features + EPSILON)
    gated, upward = gated * inverse, upward * inverse
    active = (gated / (1.0 + jnp.exp(-gated)) * upward).astype(BF16)
    active_ref[...] = active
    produce(quarter, active, down_ref, side, sent_ref)


def produce(quarter, active, down_ref, which, ref):
    for o in range(2):
        value = dot(active, down_ref[0, :, strip(2 * o + which, quarter)]).astype(BF16)
        ref[:, o * quarter : (o + 1) * quarter] = value[: ref.shape[0]]


def kept_kernel(quarter, active_ref, down_ref, kept_ref):
    produce(quarter, active_ref[...], down_ref, 1 - lax.axis_index("tensor") % 2, kept_ref)


def near_kernel(quarter, experts, kept_ref, near_ref, own_ref, far_ref, rest_ref):
    o = lax.axis_index("tensor") // 2
    main, rest = experts * MAIN, rest_ref.shape[0]

    def total(index):
        columns = strip(index, quarter)
        value = kept_ref[:, columns].astype(F32) + near_ref[:, columns].astype(F32)
        return value[:main], pack(value[main:], experts)

    value, tiles = total(1 - o)
    value, tiles = value.astype(BF16), tiles.astype(BF16)
    far_ref[:, :quarter], far_ref[:, quarter:] = value[rest:], tiles[rest:]
    rest_ref[:, :quarter], rest_ref[:, quarter:] = value[:rest], tiles[:rest]
    own_ref[:, :quarter], own_ref[:, quarter:] = total(o)


def far_kernel(start, own_ref, far_ref, *block_refs):
    for i, ref in enumerate(block_refs):
        here = slice(start + i * MAIN, start + (i + 1) * MAIN)
        ref[...] = (own_ref[here] + far_ref[i * MAIN : (i + 1) * MAIN].astype(F32)).astype(BF16)


def combine_kernel(experts, quarter, hidden_ref, mixing_ref, *refs):
    rows = hidden_ref.shape[0]
    blocks = [ref[...] for ref in refs[:experts]][::-1]
    last = jnp.concatenate(unpack([block[:, quarter:] for block in blocks], quarter // LANES), axis=1)
    slots = jnp.concatenate([*[block[:, :quarter] for block in blocks], last], axis=0)
    both = dot(mixing_ref[:, : slots.shape[0]], slots)
    refs[-1][...] = hidden_ref[...] + both[:rows] + both[rows:]


def local_kernels(residual, attention_part, norm_gain, expert_ids, gate_weights, w_gate, w_up, w_down):
    rows, features = residual.shape
    experts = lax.axis_size("expert")
    quarter = features // 4
    width = 2 * quarter
    chunks = width // LANES
    steps = range(1, experts)
    part = attention_part[0]
    near = xor_permute(part, "tensor", 1)
    before, spread = call(
        functools.partial(constant_kernel, rows), (out((rows, rows), BF16), out((rows, rows * chunks), BF16))
    )
    table, slots, tails, mixing = call(
        functools.partial(table_kernel, experts, rows, chunks),
        (
            out((experts * MAIN, rows), BF16),
            out((rows, LANES), F32),
            out((experts * MAIN, rows * chunks), BF16),
            out((2 * rows, LANES), BF16),
        ),
        before,
        spread,
        expert_ids.T,
        gate_weights.T,
    )
    chip, chip_sent = call(
        functools.partial(chip_kernel, quarter), (out((rows, width), F32), out((rows, width), BF16)), part, near, mixing
    )
    far = xor_permute(chip_sent, "tensor", 2)
    block = out((MAIN, width + LANES), BF16)
    hidden, *blocks = call(
        functools.partial(dispatch_kernel, quarter, experts),
        (out((rows, quarter), F32), *[block] * experts),
        residual,
        chip,
        far,
        norm_gain[None],
        table,
        slots,
        tails,
    )
    arrived = [*[xor_permute(blocks[k], "expert", k) for k in reversed(steps)], blocks[0]]
    packed = out((experts * MAIN, width + LANES), BF16)
    (arrived,) = call(functools.partial(pack_kernel, experts), (packed,), *arrived, flops=0)
    other = xor_permute(arrived, "tensor", 1)
    main, slot_count = experts * MAIN, (experts + 1) * MAIN
    packed_width, used = quarter + LANES, main + 8
    hidden_count = w_gate.shape[2]
    sums = out((slot_count, hidden_count), F32)
    gated, upward = call(functools.partial(own_kernel, quarter, experts), (sums, sums), arrived, w_gate, w_up)
    active, sent = call(
        functools.partial(other_kernel, quarter, experts),
        (out((slot_count, hidden_count), BF16), out((used, width), BF16)),
        arrived,
        other,
        gated,
        upward,
        w_gate,
        w_up,
        w_down,
    )
    (kept,) = call(functools.partial(kept_kernel, quarter), (out((used, width), BF16),), active, w_down)
    near = xor_permute(sent, "tensor", 1)
    early = 2
    rest = main - early * MAIN
    own, far, others = call(
        functools.partial(near_kernel, quarter, experts),
        (out((main, packed_width), F32), out((main - rest, packed_width), BF16), out((rest, packed_width), BF16)),
        kept,
        near,
    )
    far, others = xor_permute(far, "tensor", 2), xor_permute(others, "tensor", 2)
    block = out((MAIN, packed_width), BF16)
    farthest = call(functools.partial(far_kernel, rest), [block] * early, own, far)
    blocks = [*call(functools.partial(far_kernel, 0), [block] * (experts - early), own, others), *farthest]
    blocks = [*[cross_permute(blocks[k], k) for k in reversed(steps)], xor_permute(blocks[0], "tensor", 1)]
    (result,) = call(
        functools.partial(combine_kernel, experts, quarter), (out((rows, quarter), F32),), hidden, mixing, *blocks
    )
    return result


def local(residual, *others):
    rows, features = residual.shape
    fits = lax.axis_size("tensor") == 4 and lax.axis_size("expert") == 4 and rows % 16 == 0 and rows <= LANES
    quarter = features // 4
    if fits and quarter % LANES == 0 and 2 * quarter // LANES <= MAIN - 2:
        return local_kernels(residual, *others)
    return local_general(residual, *others)


def local_general(residual, attention_part, norm_gain, expert_ids, gate_weights, w_gate, w_up, w_down):
    rows, features = residual.shape
    tensor_count = lax.axis_size("tensor")
    expert_count = lax.axis_size("expert")
    tensor = lax.axis_index("tensor")
    expert = lax.axis_index("expert")
    quarter = features // tensor_count
    outer = tensor_count // 2
    side = tensor % 2

    def strips(value):
        shaped = value.reshape(value.shape[0], outer, 2, quarter)
        return lax.dynamic_index_in_dim(shaped, side, 2, keepdims=False)

    part = attention_part[0]
    near = xor_permute(part, "tensor", 1)
    chip = strips(part.astype(jnp.float32) + near.astype(jnp.float32))
    chip_sent = chip.astype(jnp.bfloat16)
    far = [xor_permute(chip_sent, "tensor", 2 * step) for step in range(1, outer)]

    relative = expert_ids ^ expert
    blocks = jnp.arange(expert_count, dtype=jnp.int32)
    chosen = relative[:, :, None] == blocks[None, None, :]
    named = jnp.any(chosen, axis=1)
    gates = jnp.sum(jnp.where(chosen, gate_weights[:, :, None], 0.0), axis=1)
    below = jnp.arange(rows)[:, None] > jnp.arange(rows)[None, :]
    position = jnp.dot(below.astype(jnp.bfloat16), named.astype(jnp.bfloat16), preferred_element_type=jnp.float32)
    slots = jnp.arange(CAP, dtype=jnp.float32)
    table = (position.T[:, None, :] == slots[None, :, None]) & named.T[:, None, :]
    mixing = jnp.where(table, gates.T[:, None, :], 0.0).reshape(expert_count * CAP, rows)
    table = table.astype(jnp.bfloat16)

    hidden = strips(residual) + chip
    for value in far:
        hidden = hidden + value.astype(jnp.float32)
    squares = jnp.sum(hidden * hidden, axis=(1, 2))
    high, low = split_pair(squares)
    extra = jnp.zeros((rows, 128), jnp.bfloat16).at[:, 0].set(high).at[:, 1].set(low)
    gained = (hidden * strips(norm_gain[None])).astype(jnp.bfloat16).reshape(rows, outer * quarter)
    sent = jnp.concatenate([gained, extra], axis=1)
    arrived = []
    for step in range(expert_count):
        block = jnp.dot(table[step], sent, preferred_element_type=jnp.float32).astype(jnp.bfloat16)
        arrived.append(xor_permute(block, "expert", step) if step else block)
    other = [xor_permute(block, "tensor", 1) for block in arrived]
    arrived, other = jnp.concatenate(arrived, axis=0), jnp.concatenate(other, axis=0)

    def columns(value):
        return value[:, : outer * quarter].reshape(-1, outer, quarter)

    first = jnp.where(side == 0, arrived, other)
    second = jnp.where(side == 0, other, arrived)
    inputs = jnp.stack([columns(first), columns(second)], axis=2).reshape(-1, features)
    tails = (arrived[:, outer * quarter :].astype(jnp.float32), other[:, outer * quarter :].astype(jnp.float32))
    total = tails[0][:, 0] + tails[0][:, 1] + tails[1][:, 0] + tails[1][:, 1]
    inverse = lax.rsqrt(total / features + EPSILON)[:, None]
    gated = jnp.dot(inputs, w_gate[0], preferred_element_type=jnp.float32) * inverse
    upward = jnp.dot(inputs, w_up[0], preferred_element_type=jnp.float32) * inverse
    active = (jax.nn.silu(gated) * upward).astype(jnp.bfloat16)
    produced = jnp.dot(active, w_down[0], preferred_element_type=jnp.float32)

    def own_columns(index):
        return lax.dynamic_slice_in_dim(produced, index * quarter, quarter, 1)

    reduced = own_columns(tensor)
    for step in range(1, tensor_count):
        piece = own_columns(tensor ^ step).astype(jnp.bfloat16)
        reduced = reduced + xor_permute(piece, "tensor", step).astype(jnp.float32)
    reduced = reduced.astype(jnp.bfloat16).reshape(expert_count, CAP, quarter)
    returned = [xor_permute(reduced[k], "expert", k) if k else reduced[k] for k in range(expert_count)]
    returned = jnp.concatenate(returned, axis=0)
    high, low = split_pair(mixing)
    dims = (((0,), (0,)), ((), ()))
    combined = lax.dot_general(high, returned, dims, preferred_element_type=jnp.float32)
    combined = combined + lax.dot_general(low, returned, dims, preferred_element_type=jnp.float32)
    return lax.dynamic_index_in_dim(hidden, tensor // 2, 1, keepdims=False) + combined


def solution(mesh):
    in_specs = (
        P(("group", "expert"), None),
        P("tensor", ("group", "expert"), None),
        P(),
        P(("group", "expert"), None),
        P(("group", "expert"), None),
        P("expert", None, "tensor"),
        P("expert", None, "tensor"),
        P("expert", "tensor", None),
    )
    out_specs = P(("group", "expert"), "tensor")
    return jax.shard_map(local, mesh=mesh, in_specs=in_specs, out_specs=out_specs, check_vma=False)
```
